32 devices in a mesh: row: 4 (over y, x), col: 8 (over z, core).
Axes of the slice: x: 2, y: 2, z: 4, core: 2. Of those that a mesh axis runs over, the one named last changes fastest.
Arguments:
- grad_out: bfloat16 [1536, 8192], P('row', 'col'), may hold values from -6 to 6
- gate_act: bfloat16 [1536, 28672], P('row', 'col'), may hold values from -6 to 6
- up_act: bfloat16 [1536, 28672], P('row', 'col'), may hold values from -6 to 6
- down_weight: bfloat16 [28672, 8192], P('col', 'row'), may hold values from -0.0625 to 0.0625
Outputs:
- grad_gate: bfloat16 [1536, 28672], P('row', 'col')
- grad_up: bfloat16 [1536, 28672], P('row', 'col')
- grad_weight: float32 [28672, 8192], P('col', 'row')
The draws below stay inside these ranges and needn't reach their ends.
All inputs are finite; a program needn't handle non-finite values.
Results may differ from the reference program's by a relative error of at most 0.0028.
Values may be sent and summed in bfloat16 or wider, within the bound.
No kernel may reach another device: no remote copies, remote signals or barrier semaphores. Data moves between devices by JAX's collectives and lax.ppermute only.
A program may use at most 192 MiB of HBM per device.

```python
import jax
import jax.numpy as jnp

D = 8192
FF = 28672
TOKENS = 1536


def levels(key, extent, cuts, low, top_value):
    level, own = 1.0, jax.random.fold_in(key, 6)
    for axis_at, parts in cuts:
        steps = jnp.exp(jax.random.uniform(jax.random.fold_in(own, axis_at), (parts,), jnp.float32, low / len(cuts), top_value / len(cuts)))
        level = level * jnp.repeat(steps, extent[axis_at] // parts).reshape([-1 if axis == axis_at else 1 for axis in range(len(extent))])
    return level


def centred(stream_key, dims, deviation, reach, shards=(), kind=jnp.bfloat16):
    loudness = levels(stream_key, dims, shards, -0.22, 0.18) if shards else 1.0
    entries = jax.random.normal(stream_key, dims, jnp.float32) * deviation * loudness
    return jnp.minimum(jnp.maximum(entries, -reach), reach).astype(kind)


def setup_inputs(seed: int = 0) -> dict:
    arg_keys = jax.random.split(jax.random.key(seed), 5)
    grad_out = centred(arg_keys[0], (TOKENS, D), 1.0, 6.0, ((0, 4), (1, 8)))
    gate_act = centred(arg_keys[1], (TOKENS, FF), 1.5, 6.0, ((0, 4), (1, 8)))
    up_act = centred(arg_keys[2], (TOKENS, FF), 1.0, 6.0, ((0, 4), (1, 8)))
    down_weight = centred(arg_keys[3], (FF, D), D ** -0.5, 0.0625, ((0, 8), (1, 4)))
    return dict(grad_out=grad_out, gate_act=gate_act, up_act=up_act, down_weight=down_weight)


def reference(grad_out, gate_act, up_act, down_weight):
    grad_hidden = jnp.dot(grad_out, down_weight.T, preferred_element_type=jnp.float32)
    gate_value = gate_act.astype(jnp.float32)
    up_value = up_act.astype(jnp.float32)
    sigmoid_gate = jax.nn.sigmoid(gate_value)
    swish = gate_value * sigmoid_gate
    grad_gate = (grad_hidden * up_value * sigmoid_gate * (1.0 + gate_value * (1.0 - sigmoid_gate))).astype(jnp.bfloat16)
    grad_up = (grad_hidden * swish).astype(jnp.bfloat16)
    hidden = (swish * up_value).astype(jnp.bfloat16)
    grad_weight = jnp.dot(hidden.T, grad_out, preferred_element_type=jnp.float32)
    return grad_gate, grad_up, grad_weight
```

```python
import jax
import jax.numpy as jnp
from jax import lax
from jax.sharding import PartitionSpec as P

CHUNKS = 4
BOTH = ("row", "col")


def exchange_pairs(rows, cols, step):
    bits = rows.bit_length() - 1
    return [
        (r * cols + c, (r ^ (1 << ((step + c) % bits))) * cols + c)
        for r in range(rows)
        for c in range(cols)
    ]


def token_order(rows, col_at):
    bits = rows.bit_length() - 1
    offsets = []
    for place in range(rows):
        offset = 0
        for step in range(bits):
            if place >> step & 1:
                offset = offset + (1 << ((step + col_at) % bits))
        offsets.append(offset)
    return offsets


def collect_tokens(grad_out, rows, cols):
    share = cols // rows
    part = grad_out.shape[0] // share
    lane = lax.axis_index("col") % share
    arrived = []
    for shift in range(share):
        piece = lax.dynamic_slice_in_dim(grad_out, (lane + shift) % share * part, part, 0)
        pairs = [
            (
                r * cols + to * share + k,
                to * cols + (r ^ to) * share + (k + shift) % share,
            )
            for r in range(rows)
            for to in range(rows)
            for k in range(share)
        ]
        arrived.append(lax.ppermute(piece, BOTH, pairs))
    arrived = jnp.stack(arrived)
    mine = jnp.concatenate(
        [
            lax.dynamic_index_in_dim(arrived, (lane - k) % share, 0, keepdims=False)
            for k in range(share)
        ],
        axis=1,
    )
    return lax.all_gather(mine, "col", axis=0, tiled=True)


def on_device(grad_out, gate_act, up_act, down_weight):
    rows, cols = lax.axis_size("row"), lax.axis_size("col")
    steps = rows.bit_length() - 1
    tokens = grad_out.shape[0]
    pairs = [exchange_pairs(rows, cols, step) for step in range(steps)]

    gate_value = gate_act.astype(jnp.float32)
    up_value = up_act.astype(jnp.float32)
    sigmoid_gate = jax.nn.sigmoid(gate_value)
    hidden = (gate_value * sigmoid_gate * up_value).astype(jnp.bfloat16)

    grads = collect_tokens(grad_out, rows, cols)
    offsets = token_order(rows, lax.axis_index("col"))
    places = sorted(
        range(rows), key=lambda place: [1 - (place >> step & 1) for step in range(steps)]
    )
    grads = jnp.concatenate(
        [
            lax.dynamic_slice_in_dim(grads, offsets[place] * tokens, tokens, 0)
            for place in places
        ],
        axis=0,
    )

    gathered = [hidden]
    for step in range(steps):
        gathered = gathered + [lax.ppermute(block, BOTH, pairs[step]) for block in gathered]
    hidden_all = jnp.concatenate([gathered[place] for place in places], axis=0)

    grads, gate_act, up_act, *_ = lax.optimization_barrier(
        (grads, gate_act, up_act, *gathered[1 : rows // 2 + 1])
    )
    grad_weight = lax.dot_general(
        hidden_all, grads, (((0,), (0,)), ((), ())), preferred_element_type=jnp.float32
    )

    width = down_weight.shape[0] // CHUNKS
    half = rows // 2 * tokens
    sums = []
    for chunk in range(CHUNKS):
        weight = lax.slice_in_dim(down_weight, chunk * width, (chunk + 1) * width, axis=0)

        def partial(start, stop):
            return lax.dot_general(
                grads[start:stop],
                weight,
                (((1,), (1,)), ((), ())),
                preferred_element_type=jnp.float32,
            )

        came = lax.ppermute(partial(0, half).astype(jnp.bfloat16), BOTH, pairs[0])
        if chunk == CHUNKS - 1:
            came, grad_weight = lax.optimization_barrier((came, grad_weight))
        if chunk == 0:
            grads, *_ = lax.optimization_barrier((grads, *gathered))
        start, arrived = half, [came]
        for step in range(1, steps):
            size = (rows * tokens - start) // 2
            total = partial(start, start + size)
            for block in arrived:
                total = total + block[:size].astype(jnp.float32)
            arrived = [block[size:] for block in arrived]
            arrived.append(lax.ppermute(total.astype(jnp.bfloat16), BOTH, pairs[step]))
            start += size
        total = partial(start, start + tokens)
        for block in arrived[:-1]:
            total = total + block.astype(jnp.float32)
        total, last = lax.optimization_barrier((total, arrived[-1]))
        sums.append(total + last.astype(jnp.float32))
    grad_hidden = jnp.concatenate(sums, axis=1)

    gate_value = gate_act.astype(jnp.float32)
    up_value = up_act.astype(jnp.float32)
    sigmoid_gate = jax.nn.sigmoid(gate_value)
    grad_gate = (
        grad_hidden * up_value * sigmoid_gate * (1.0 + gate_value * (1.0 - sigmoid_gate))
    ).astype(jnp.bfloat16)
    grad_up = (grad_hidden * (gate_value * sigmoid_gate)).astype(jnp.bfloat16)
    return (grad_gate, grad_up, grad_weight)


def solution(mesh):
    placed = (P("row", "col"), P("row", "col"), P("row", "col"), P("col", "row"))
    return jax.shard_map(
        on_device,
        mesh=mesh,
        in_specs=placed,
        out_specs=(P("row", "col"), P("row", "col"), P("col", "row")),
        check_vma=False,
    )
```

```python
import jax
import jax.numpy as jnp
from jax import lax
from jax.sharding import PartitionSpec as P

CHUNKS = 2
BOTH = ("row", "col")


def exchange_pairs(rows, cols, step):
    bits = rows.bit_length() - 1
    return [
        (r * cols + c, (r ^ (1 << ((step + c) % bits))) * cols + c)
        for r in range(rows)
        for c in range(cols)
    ]


def row_offset(rows, place, turn):
    bits = rows.bit_length() - 1
    return sum(1 << ((step + turn) % bits) for step in range(bits) if place >> step & 1)


def collect_tokens(grad_out, hidden, sent, rows, cols):
    share = cols // rows
    part = grad_out.shape[0] // cols
    row, col = lax.axis_index("row"), lax.axis_index("col")
    plane, lane = col // share, col % share

    pieces = grad_out.reshape(rows, share, part, grad_out.shape[1])
    arrived = []
    for shift in range(share):
        piece = lax.dynamic_index_in_dim(pieces, (lane + shift) % share, 1, keepdims=False)
        if shift:
            pairs = [
                (p * share + k, p * share + (k + shift) % share)
                for p in range(rows)
                for k in range(share)
            ]
            piece = lax.ppermute(piece, "col", pairs)
        arrived.append(piece)
    arrived = jnp.stack(arrived)
    mine = jnp.concatenate(
        [
            lax.dynamic_index_in_dim(arrived, (lane - k) % share, 0, keepdims=False)
            for k in range(share)
        ],
        axis=2,
    )

    mine, hidden = lax.optimization_barrier((mine, hidden))

    held = []
    for flip in range(rows):
        piece = lax.dynamic_index_in_dim(mine, plane ^ flip, 0, keepdims=False)
        if flip:
            pairs = [(c, (c // share ^ flip) * share + c % share) for c in range(cols)]
            piece = lax.ppermute(piece, "col", pairs)
        held.append(piece)
    held, _ = lax.optimization_barrier((jnp.stack(held), sent))

    blocks = []
    for flip in range(rows):
        piece = lax.dynamic_index_in_dim(held, row ^ flip ^ plane, 0, keepdims=False)
        if flip:
            piece = lax.ppermute(piece, "row", [(r, r ^ flip) for r in range(rows)])
        blocks.append(piece)
    first = lax.all_gather(blocks[-1], "col", axis=0, tiled=True)
    first, *rest = lax.optimization_barrier((first, *blocks[:-1]))
    rest = lax.all_gather(jnp.stack(rest), "col", axis=1, tiled=True)
    return [rest[flip] for flip in range(rows - 1)] + [first]


def on_device(grad_out, gate_act, up_act, down_weight):
    rows, cols = lax.axis_size("row"), lax.axis_size("col")
    steps = rows.bit_length() - 1
    pairs = [exchange_pairs(rows, cols, step) for step in range(steps)]

    gate_value = gate_act.astype(jnp.float32)
    up_value = up_act.astype(jnp.float32)
    sigmoid_gate = jax.nn.sigmoid(gate_value)
    hidden = (gate_value * sigmoid_gate * up_value).astype(jnp.bfloat16)
    gathered = []
    for half in jnp.split(hidden, 2):
        parts = [half]
        for step in range(steps):
            parts = parts + [lax.ppermute(part, BOTH, pairs[step]) for part in parts]
        gathered.append(parts)

    blocks = collect_tokens(grad_out, hidden, gathered[0][1], rows, cols)
    early = [part for parts in gathered for part in parts[1 : rows // 2 + 1]]
    blocks[-1], gate_act, up_act, *_ = lax.optimization_barrier(
        (blocks[-1], gate_act, up_act, *early)
    )
    turn = lax.axis_index("col") % steps
    grads = [
        lax.select_n(turn, *(blocks[row_offset(rows, place, t)] for t in range(steps)))
        if 0 < place < rows - 1
        else blocks[place]
        for place in range(rows)
    ]
    grad_weight = lax.dot_general(
        jnp.concatenate([part for place in zip(*gathered) for part in place], axis=0),
        jnp.concatenate(grads, axis=0),
        (((0,), (0,)), ((), ())),
        preferred_element_type=jnp.float32,
    )

    width = down_weight.shape[0] // CHUNKS
    weights = [
        lax.slice_in_dim(down_weight, chunk * width, (chunk + 1) * width, axis=0)
        for chunk in range(CHUNKS)
    ]
    came = [[[] for _ in range(rows)] for _ in range(CHUNKS)]

    def partial(chunk, place):
        return lax.dot_general(
            grads[place],
            weights[chunk],
            (((1,), (1,)), ((), ())),
            preferred_element_type=jnp.float32,
        )

    for step in range(steps):
        for place in reversed(range(rows)):
            if place & ((1 << step) - 1) or not place >> step & 1:
                continue
            for chunk in range(CHUNKS):
                arrived = came[chunk][place]
                if step == steps - 1 and chunk == CHUNKS - 1:
                    arrived[0], grad_weight = lax.optimization_barrier((arrived[0], grad_weight))
                total = partial(chunk, place)
                for block in arrived:
                    total = total + block.astype(jnp.float32)
                sent = lax.ppermute(total.astype(jnp.bfloat16), BOTH, pairs[step])
                came[chunk][place ^ (1 << step)].append(sent)
    sums = []
    for chunk in range(CHUNKS):
        total, *arrived = lax.optimization_barrier((partial(chunk, 0), *came[chunk][0]))
        for block in arrived:
            total = total + block.astype(jnp.float32)
        sums.append(total)
    grad_hidden = jnp.concatenate(sums, axis=1)

    gate_value = gate_act.astype(jnp.float32)
    up_value = up_act.astype(jnp.float32)
    sigmoid_gate = jax.nn.sigmoid(gate_value)
    grad_gate = (
        grad_hidden * up_value * sigmoid_gate * (1.0 + gate_value * (1.0 - sigmoid_gate))
    ).astype(jnp.bfloat16)
    grad_up = (grad_hidden * (gate_value * sigmoid_gate)).astype(jnp.bfloat16)
    return (grad_gate, grad_up, grad_weight)


def solution(mesh):
    placed = (P("row", "col"), P("row", "col"), P("row", "col"), P("col", "row"))
    return jax.shard_map(
        on_device,
        mesh=mesh,
        in_specs=placed,
        out_specs=(P("row", "col"), P("row", "col"), P("col", "row")),
        check_vma=False,
    )
```

```python
import jax
import jax.numpy as jnp
from jax import lax
from jax.sharding import PartitionSpec as P

CHUNKS = 2
BOTH = ("row", "col")


def exchange_pairs(rows, cols, step):
    bits = rows.bit_length() - 1
    return [
        (r * cols + c, (r ^ (1 << ((step + c) % bits))) * cols + c)
        for r in range(rows)
        for c in range(cols)
    ]


def row_offset(rows, place, turn):
    bits = rows.bit_length() - 1
    return sum(1 << ((step + turn) % bits) for step in range(bits) if place >> step & 1)


def collect_tokens(grad_out, front, front_came, rows, cols):
    share = cols // rows
    part = grad_out.shape[0] // cols
    row, col = lax.axis_index("row"), lax.axis_index("col")
    plane, lane = col // share, col % share

    pieces = grad_out.reshape(rows, share, part, grad_out.shape[1])
    arrived = []
    for shift in range(share):
        piece = lax.dynamic_index_in_dim(pieces, (lane + shift) % share, 1, keepdims=False)
        if shift:
            pairs = [
                (p * share + k, p * share + (k + shift) % share)
                for p in range(rows)
                for k in range(share)
            ]
            piece = lax.ppermute(piece, "col", pairs)
        arrived.append(piece)
    arrived = jnp.stack(arrived)
    mine = jnp.concatenate(
        [
            lax.dynamic_index_in_dim(arrived, (lane - k) % share, 0, keepdims=False)
            for k in range(share)
        ],
        axis=2,
    )

    mine, _ = lax.optimization_barrier((mine, front))

    held = []
    for flip in range(rows):
        piece = lax.dynamic_index_in_dim(mine, plane ^ flip, 0, keepdims=False)
        if flip:
            pairs = [(c, (c // share ^ flip) * share + c % share) for c in range(cols)]
            piece = lax.ppermute(piece, "col", pairs)
        held.append(piece)
    held, _ = lax.optimization_barrier((jnp.stack(held), front_came))

    blocks = [None] * rows
    for flip in reversed(range(rows)):
        piece = lax.dynamic_index_in_dim(held, row ^ flip ^ plane, 0, keepdims=False)
        if flip < rows - 1:
            piece, _ = lax.optimization_barrier((piece, blocks[-1]))
        if flip:
            piece = lax.ppermute(piece, "row", [(r, r ^ flip) for r in range(rows)])
        blocks[flip] = piece
    first = lax.all_gather(blocks[-1], "col", axis=0, tiled=True)
    rest = lax.all_gather(jnp.stack(blocks[:-1]), "col", axis=1, tiled=True)
    return [rest[flip] for flip in range(rows - 1)] + [first]


def on_device(grad_out, gate_act, up_act, down_weight):
    rows, cols = lax.axis_size("row"), lax.axis_size("col")
    steps = rows.bit_length() - 1
    pairs = [exchange_pairs(rows, cols, step) for step in range(steps)]

    def activation(gate, up):
        gate = gate.astype(jnp.float32)
        return (gate * jax.nn.sigmoid(gate) * up.astype(jnp.float32)).astype(jnp.bfloat16)

    gate_halves, up_halves = jnp.split(gate_act, 2), jnp.split(up_act, 2)
    front = activation(gate_halves[0], up_halves[0])
    front_came = lax.ppermute(front, BOTH, pairs[0])
    front, *late = lax.optimization_barrier((front, gate_halves[1], up_halves[1]))
    back = activation(*late)
    gathered = [
        jnp.concatenate([front, back]),
        jnp.concatenate([front_came, lax.ppermute(back, BOTH, pairs[0])]),
    ]
    gathered[0], _ = lax.optimization_barrier((gathered[0], front_came))
    for step in range(1, steps):
        gathered = gathered + [lax.ppermute(part, BOTH, pairs[step]) for part in gathered]

    blocks = collect_tokens(grad_out, front, front_came, rows, cols)
    gate_act, up_act, _ = lax.optimization_barrier((gate_act, up_act, front_came))
    turn = lax.axis_index("col") % steps
    grads = [
        lax.select_n(turn, *(blocks[row_offset(rows, place, t)] for t in range(steps)))
        if 0 < place < rows - 1
        else blocks[place]
        for place in range(rows)
    ]
    width = down_weight.shape[0] // CHUNKS
    weights = [
        lax.slice_in_dim(down_weight, chunk * width, (chunk + 1) * width, axis=0)
        for chunk in range(CHUNKS)
    ]
    came = [[[] for _ in range(rows)] for _ in range(CHUNKS)]

    def partial(chunk, place):
        return lax.dot_general(
            grads[place],
            weights[chunk],
            (((1,), (1,)), ((), ())),
            preferred_element_type=jnp.float32,
        )

    for step in range(steps):
        for place in reversed(range(rows)):
            if place & ((1 << step) - 1) or not place >> step & 1:
                continue
            for chunk in range(CHUNKS):
                arrived = came[chunk][place]
                if step == steps - 1:
                    if chunk == 0:
                        every_token, _ = lax.optimization_barrier(
                            (jnp.concatenate(grads, axis=0), total)
                        )
                        grad_weight = lax.dot_general(
                            jnp.concatenate(gathered, axis=0),
                            every_token,
                            (((0,), (0,)), ((), ())),
                            preferred_element_type=jnp.float32,
                        )
                    arrived[0], came[chunk][0][-1] = lax.optimization_barrier(
                        (arrived[0], came[chunk][0][-1])
                    )
                    if chunk == CHUNKS - 1:
                        arrived[0], grad_weight = lax.optimization_barrier(
                            (arrived[0], grad_weight)
                        )
                total = partial(chunk, place)
                for block in arrived:
                    total = total + block.astype(jnp.float32)
                total = total.astype(jnp.bfloat16)
                if place == rows - 1:
                    total, _ = lax.optimization_barrier((total, gathered[rows // 2]))
                elif step == 0:
                    total, _ = lax.optimization_barrier((total, gathered[rows - 1]))
                sent = lax.ppermute(total, BOTH, pairs[step])
                came[chunk][place ^ (1 << step)].append(sent)
    sums = []
    for chunk in range(CHUNKS):
        total, *arrived = lax.optimization_barrier((partial(chunk, 0), *came[chunk][0]))
        for block in arrived:
            total = total + block.astype(jnp.float32)
        sums.append(total)
    grad_hidden = jnp.concatenate(sums, axis=1)

    gate_value = gate_act.astype(jnp.float32)
    up_value = up_act.astype(jnp.float32)
    sigmoid_gate = jax.nn.sigmoid(gate_value)
    grad_gate = (
        grad_hidden * up_value * sigmoid_gate * (1.0 + gate_value * (1.0 - sigmoid_gate))
    ).astype(jnp.bfloat16)
    grad_up = (grad_hidden * (gate_value * sigmoid_gate)).astype(jnp.bfloat16)
    return (grad_gate, grad_up, grad_weight)


def solution(mesh):
    placed = (P("row", "col"), P("row", "col"), P("row", "col"), P("col", "row"))
    return jax.shard_map(
        on_device,
        mesh=mesh,
        in_specs=placed,
        out_specs=(P("row", "col"), P("row", "col"), P("col", "row")),
        check_vma=False,
    )
```

```python
import jax
import jax.numpy as jnp
from jax import lax
from jax.sharding import PartitionSpec as P

CHUNKS = 2
BOTH = ("row", "col")


def exchange_pairs(rows, cols, step):
    bits = rows.bit_length() - 1
    return [
        (r * cols + c, (r ^ (1 << ((step + c) % bits))) * cols + c)
        for r in range(rows)
        for c in range(cols)
    ]


def row_offset(rows, place, turn):
    bits = rows.bit_length() - 1
    return sum(1 << ((step + turn) % bits) for step in range(bits) if place >> step & 1)


def collect_tokens(grad_out, front, front_came, rows, cols):
    share = cols // rows
    part = grad_out.shape[0] // cols
    row, col = lax.axis_index("row"), lax.axis_index("col")
    plane, lane = col // share, col % share

    pieces = grad_out.reshape(rows, share, part, grad_out.shape[1])
    arrived = []
    for shift in range(share):
        piece = lax.dynamic_index_in_dim(pieces, (lane + shift) % share, 1, keepdims=False)
        if shift:
            pairs = [
                (p * share + k, p * share + (k + shift) % share)
                for p in range(rows)
                for k in range(share)
            ]
            piece = lax.ppermute(piece, "col", pairs)
        arrived.append(piece)
    arrived = jnp.stack(arrived)
    mine = jnp.concatenate(
        [
            lax.dynamic_index_in_dim(arrived, (lane - k) % share, 0, keepdims=False)
            for k in range(share)
        ],
        axis=2,
    )

    mine, _ = lax.optimization_barrier((mine, front))

    held = []
    for flip in range(rows):
        piece = lax.dynamic_index_in_dim(mine, plane ^ flip, 0, keepdims=False)
        if flip:
            pairs = [(c, (c // share ^ flip) * share + c % share) for c in range(cols)]
            piece = lax.ppermute(piece, "col", pairs)
        held.append(piece)
    held, _ = lax.optimization_barrier((jnp.stack(held), front_came))

    blocks = [None] * rows
    for flip in reversed(range(rows)):
        piece = lax.dynamic_index_in_dim(held, row ^ flip ^ plane, 0, keepdims=False)
        if flip < rows - 1:
            piece, _ = lax.optimization_barrier((piece, blocks[-1]))
        if flip:
            piece = lax.ppermute(piece, "row", [(r, r ^ flip) for r in range(rows)])
        blocks[flip] = piece
    first = lax.all_gather(blocks[-1], "col", axis=0, tiled=True)
    rest = lax.all_gather(jnp.stack(blocks[:-1]), "col", axis=1, tiled=True)
    return [rest[flip] for flip in range(rows - 1)] + [first]


def on_device(grad_out, gate_act, up_act, down_weight):
    rows, cols = lax.axis_size("row"), lax.axis_size("col")
    steps = rows.bit_length() - 1
    pairs = [exchange_pairs(rows, cols, step) for step in range(steps)]

    def activation(gate, up):
        gate = gate.astype(jnp.float32)
        return (gate * jax.nn.sigmoid(gate) * up.astype(jnp.float32)).astype(jnp.bfloat16)

    gate_halves, up_halves = jnp.split(gate_act, 2), jnp.split(up_act, 2)
    front = activation(gate_halves[0], up_halves[0])
    front_came = lax.ppermute(front, BOTH, pairs[0])
    front, *late = lax.optimization_barrier((front, gate_halves[1], up_halves[1]))
    back = activation(*late)
    gathered = [
        jnp.concatenate([front, back]),
        jnp.concatenate([front_came, lax.ppermute(back, BOTH, pairs[0])]),
    ]
    gathered[0], _ = lax.optimization_barrier((gathered[0], front_came))
    for step in range(1, steps - 1):
        gathered = gathered + [lax.ppermute(part, BOTH, pairs[step]) for part in gathered]
    gathered.append(lax.ppermute(gathered[0], BOTH, pairs[-1]))

    blocks = collect_tokens(grad_out, front, front_came, rows, cols)
    gate_act, up_act, _ = lax.optimization_barrier((gate_act, up_act, front_came))
    turn = lax.axis_index("col") % steps
    grads = [
        lax.select_n(turn, *(blocks[row_offset(rows, place, t)] for t in range(steps)))
        if 0 < place < rows - 1
        else blocks[place]
        for place in range(rows)
    ]
    width = down_weight.shape[0] // CHUNKS
    weights = [
        lax.slice_in_dim(down_weight, chunk * width, (chunk + 1) * width, axis=0)
        for chunk in range(CHUNKS)
    ]
    came = [[[] for _ in range(rows)] for _ in range(CHUNKS)]

    def partial(chunk, place):
        return lax.dot_general(
            grads[place],
            weights[chunk],
            (((1,), (1,)), ((), ())),
            preferred_element_type=jnp.float32,
        )

    for step in range(steps):
        for place in reversed(range(rows)):
            if place & ((1 << step) - 1) or not place >> step & 1:
                continue
            for chunk in range(CHUNKS):
                arrived = came[chunk][place]
                if step == steps - 1:
                    if chunk == 0:
                        arrived[0], _ = lax.optimization_barrier((arrived[0], total))
                    if chunk == CHUNKS - 1:
                        every_token, _ = lax.optimization_barrier(
                            (jnp.concatenate(grads, axis=0), total)
                        )
                        grad_weight = lax.dot_general(
                            jnp.concatenate(gathered, axis=0),
                            every_token,
                            (((0,), (0,)), ((), ())),
                            preferred_element_type=jnp.float32,
                        )
                        arrived[0], grad_weight = lax.optimization_barrier(
                            (arrived[0], grad_weight)
                        )
                total = partial(chunk, place)
                for block in arrived:
                    total = total + block.astype(jnp.float32)
                total = total.astype(jnp.bfloat16)
                if place == rows - 1:
                    total, _ = lax.optimization_barrier((total, gathered[rows // 2]))
                    if chunk == CHUNKS - 1:
                        for part in gathered[1 : rows // 2]:
                            part, _ = lax.optimization_barrier((part, total))
                            gathered.append(lax.ppermute(part, BOTH, pairs[-1]))
                sent = lax.ppermute(total, BOTH, pairs[step])
                came[chunk][place ^ (1 << step)].append(sent)
    sums = []
    for chunk in range(CHUNKS):
        total, *arrived = lax.optimization_barrier((partial(chunk, 0), *came[chunk][0]))
        for block in arrived:
            total = total + block.astype(jnp.float32)
        sums.append(total)
    grad_hidden = jnp.concatenate(sums, axis=1)

    gate_value = gate_act.astype(jnp.float32)
    up_value = up_act.astype(jnp.float32)
    sigmoid_gate = jax.nn.sigmoid(gate_value)
    grad_gate = (
        grad_hidden * up_value * sigmoid_gate * (1.0 + gate_value * (1.0 - sigmoid_gate))
    ).astype(jnp.bfloat16)
    grad_up = (grad_hidden * (gate_value * sigmoid_gate)).astype(jnp.bfloat16)
    return (grad_gate, grad_up, grad_weight)


def solution(mesh):
    placed = (P("row", "col"), P("row", "col"), P("row", "col"), P("col", "row"))
    return jax.shard_map(
        on_device,
        mesh=mesh,
        in_specs=placed,
        out_specs=(P("row", "col"), P("row", "col"), P("col", "row")),
        check_vma=False,
    )
```

```python
import jax
import jax.numpy as jnp
from jax import lax
from jax.sharding import PartitionSpec as P

BOTH = ("row", "col")


def exchange_pairs(rows, cols, step):
    bits = rows.bit_length() - 1
    return [
        (r * cols + c, (r ^ (1 << ((step + c) % bits))) * cols + c)
        for r in range(rows)
        for c in range(cols)
    ]


def row_offset(rows, place, turn):
    bits = rows.bit_length() - 1
    return sum(1 << ((step + turn) % bits) for step in range(bits) if place >> step & 1)


def collect_tokens(grad_out, front, front_came, later, rows, cols):
    share = cols // rows
    part = grad_out.shape[0] // cols
    row, col = lax.axis_index("row"), lax.axis_index("col")
    plane, lane = col // share, col % share

    pieces = grad_out.reshape(rows, share, part, grad_out.shape[1])
    arrived = []
    for shift in range(share):
        piece = lax.dynamic_index_in_dim(pieces, (lane + shift) % share, 1, keepdims=False)
        if shift:
            pairs = [
                (p * share + k, p * share + (k + shift) % share)
                for p in range(rows)
                for k in range(share)
            ]
            piece = lax.ppermute(piece, "col", pairs)
        arrived.append(piece)
    arrived = jnp.stack(arrived)
    mine = jnp.concatenate(
        [
            lax.dynamic_index_in_dim(arrived, (lane - k) % share, 0, keepdims=False)
            for k in range(share)
        ],
        axis=2,
    )

    mine, _ = lax.optimization_barrier((mine, front))

    held = []
    for flip in range(rows):
        piece = lax.dynamic_index_in_dim(mine, plane ^ flip, 0, keepdims=False)
        if flip:
            pairs = [(c, (c // share ^ flip) * share + c % share) for c in range(cols)]
            piece = lax.ppermute(piece, "col", pairs)
        held.append(piece)
    held, _ = lax.optimization_barrier((jnp.stack(held), front_came))

    blocks = [None] * rows
    for flip in reversed(range(rows)):
        piece = lax.dynamic_index_in_dim(held, row ^ flip ^ plane, 0, keepdims=False)
        if flip < rows - 1:
            piece, _ = lax.optimization_barrier((piece, blocks[-1]))
        if flip:
            piece = lax.ppermute(piece, "row", [(r, r ^ flip) for r in range(rows)])
        blocks[flip] = piece
    first = lax.all_gather(blocks[-1], "col", axis=0, tiled=True)
    rest, *_ = lax.optimization_barrier((jnp.stack(blocks[:-1]), *later))
    rest = lax.all_gather(rest, "col", axis=1, tiled=True)
    return [rest[flip] for flip in range(rows - 1)] + [first]


def on_device(grad_out, gate_act, up_act, down_weight):
    rows, cols = lax.axis_size("row"), lax.axis_size("col")
    steps = rows.bit_length() - 1
    tokens = grad_out.shape[0]
    pairs = [exchange_pairs(rows, cols, step) for step in range(steps)]

    def after(value, *others):
        return lax.optimization_barrier((value, *others))[0]

    def activation(gate, up):
        gate = gate.astype(jnp.float32)
        return (gate * jax.nn.sigmoid(gate) * up.astype(jnp.float32)).astype(jnp.bfloat16)

    size = tokens * 3 // 4
    front = activation(gate_act[:size], up_act[:size])
    front_came = lax.ppermute(front, BOTH, pairs[0])
    back = activation(after(gate_act[size:], front), after(up_act[size:], front))
    back_came = lax.ppermute(after(back, front_came), BOTH, pairs[0])
    halves = jnp.split(after(jnp.concatenate([front, back]), front_came), 2)
    halves_came = [lax.ppermute(half, BOTH, pairs[-1]) for half in halves]
    gathered = [jnp.concatenate([front, back]), jnp.concatenate([front_came, back_came])]
    for step in range(1, steps - 1):
        gathered = gathered + [lax.ppermute(part, BOTH, pairs[step]) for part in gathered]
    gathered += [jnp.concatenate(halves_came)] + [
        lax.ppermute(part, BOTH, pairs[-1]) for part in gathered[1:]
    ]

    blocks = collect_tokens(grad_out, front, front_came, [back_came, halves_came[0]], rows, cols)
    turn = lax.axis_index("col") % steps
    grads = [
        lax.select_n(turn, *(blocks[row_offset(rows, place, t)] for t in range(steps)))
        if 0 < place < rows - 1
        else blocks[place]
        for place in range(rows)
    ]

    width = down_weight.shape[0]
    weights = jnp.split(down_weight, [width // 7, width // 7 + width // 2])
    chunks = range(len(weights))
    came = [[[] for _ in range(rows)] for _ in chunks]
    total = front

    def partial(chunk, place, before):
        return lax.dot_general(
            after(grads[place], before),
            weights[chunk],
            (((1,), (1,)), ((), ())),
            preferred_element_type=jnp.float32,
        )

    for step in range(steps):
        for place in reversed(range(rows)):
            if place & ((1 << step) - 1) or not place >> step & 1:
                continue
            for chunk in chunks:
                total = partial(chunk, place, total)
                for block in came[chunk][place]:
                    total = total + block.astype(jnp.float32)
                total = total.astype(jnp.bfloat16)
                if place == rows - 1 and chunk == 0:
                    total = after(total, halves_came[1], *gathered[rows // 2 + 1 :])
                sent = lax.ppermute(total, BOTH, pairs[step])
                came[chunk][place ^ (1 << step)].append(sent)

    own = []
    for chunk in chunks:
        total = partial(chunk, 0, total)
        own.append(total)

    gathered, grads, own = lax.optimization_barrier((gathered, grads, own))
    grad_weight = lax.dot_general(
        jnp.concatenate(gathered, axis=0),
        jnp.concatenate(grads, axis=0),
        (((0,), (0,)), ((), ())),
        preferred_element_type=jnp.float32,
    )
    own, grad_weight = lax.optimization_barrier((own, grad_weight))

    sums = []
    for chunk in chunks:
        total = own[chunk]
        for block in came[chunk][0]:
            total = total + block.astype(jnp.float32)
        sums.append(total)
    grad_hidden = jnp.concatenate(sums, axis=1)
    gate_value = after(gate_act, front_came).astype(jnp.float32)
    up_value = after(up_act, front_came).astype(jnp.float32)
    sigmoid_gate = jax.nn.sigmoid(gate_value)
    grad_gate = (
        grad_hidden * up_value * sigmoid_gate * (1.0 + gate_value * (1.0 - sigmoid_gate))
    ).astype(jnp.bfloat16)
    grad_up = (grad_hidden * (gate_value * sigmoid_gate)).astype(jnp.bfloat16)
    return (grad_gate, grad_up, grad_weight)


def solution(mesh):
    placed = (P("row", "col"), P("row", "col"), P("row", "col"), P("col", "row"))
    return jax.shard_map(
        on_device,
        mesh=mesh,
        in_specs=placed,
        out_specs=(P("row", "col"), P("row", "col"), P("col", "row")),
        check_vma=False,
    )
```

```python
import math

import jax
import jax.numpy as jnp
from jax import lax
from jax.experimental import pallas as pl
from jax.experimental.pallas import tpu as pltpu
from jax.sharding import PartitionSpec as P

BOTH = ("row", "col")


def exchange_pairs(rows, cols, step):
    bits = rows.bit_length() - 1
    return [
        (r * cols + c, (r ^ (1 << ((step + c) % bits))) * cols + c)
        for r in range(rows)
        for c in range(cols)
    ]


def row_offset(rows, place, turn):
    bits = rows.bit_length() - 1
    return sum(1 << ((step + turn) % bits) for step in range(bits) if place >> step & 1)


def spread_tokens(grad_out, hidden, hidden_came, rows, cols):
    share = cols // rows
    part = grad_out.shape[0] // cols
    row, col = lax.axis_index("row"), lax.axis_index("col")
    plane, lane = col // share, col % share

    pieces = grad_out.reshape(rows, share, part, grad_out.shape[1])
    arrived = []
    for shift in range(share):
        piece = lax.dynamic_index_in_dim(pieces, (lane + shift) % share, 1, keepdims=False)
        if shift:
            pairs = [
                (p * share + k, p * share + (k + shift) % share)
                for p in range(rows)
                for k in range(share)
            ]
            piece = lax.ppermute(piece, "col", pairs)
        arrived.append(piece)
    arrived = jnp.stack(arrived)
    mine = jnp.concatenate(
        [
            lax.dynamic_index_in_dim(arrived, (lane - k) % share, 0, keepdims=False)
            for k in range(share)
        ],
        axis=2,
    )

    mine, _ = lax.optimization_barrier((mine, hidden))

    held = []
    for flip in range(rows):
        piece = lax.dynamic_index_in_dim(mine, plane ^ flip, 0, keepdims=False)
        if flip:
            pairs = [(c, (c // share ^ flip) * share + c % share) for c in range(cols)]
            piece = lax.ppermute(piece, "col", pairs)
        held.append(piece)
    held, _ = lax.optimization_barrier((jnp.stack(held), hidden_came))

    blocks = [None] * rows
    for flip in reversed(range(rows)):
        piece = lax.dynamic_index_in_dim(held, row ^ flip ^ plane, 0, keepdims=False)
        if flip < rows - 1:
            piece, _ = lax.optimization_barrier((piece, blocks[-1]))
        if flip:
            piece = lax.ppermute(piece, "row", [(r, r ^ flip) for r in range(rows)])
        blocks[flip] = piece
    return blocks


def gather_tokens(blocks):
    first = lax.all_gather(blocks[-1], "col", axis=0, tiled=True)
    rest = lax.all_gather(jnp.stack(blocks[:-1]), "col", axis=1, tiled=True)
    return [rest[flip] for flip in range(len(blocks) - 1)] + [first]


def finish_kernel(own_ref, *refs):
    *came_refs, gate_ref, up_ref = refs[: len(refs) - 2]
    gate_out_ref, up_out_ref = refs[-2:]
    grad_hidden = own_ref[...]
    for came_ref in came_refs:
        grad_hidden = grad_hidden + came_ref[...].astype(jnp.float32)
    gate_value = gate_ref[...].astype(jnp.float32)
    up_value = up_ref[...].astype(jnp.float32)
    sigmoid_gate = 1.0 / (1.0 + jnp.exp(-gate_value))
    gate_out_ref[...] = (
        grad_hidden * up_value * sigmoid_gate * (1.0 + gate_value * (1.0 - sigmoid_gate))
    ).astype(jnp.bfloat16)
    up_out_ref[...] = (grad_hidden * (gate_value * sigmoid_gate)).astype(jnp.bfloat16)


def finish(own, last, whole, gate_act, up_act, outs, start, block):
    tokens, width = own.shape
    inner = pl.BlockSpec((tokens, block), lambda i: (0, i))
    outer = pl.BlockSpec((tokens, block), lambda i: (0, start // block + i))
    operands = [own, last, *whole, gate_act, up_act]
    specs = [inner] * 2 + [outer] * (len(whole) + 2)
    kernel, aliases = finish_kernel, {}
    if outs:
        aliases = {len(operands): 0, len(operands) + 1: 1}
        operands += outs
        specs += [pl.BlockSpec(memory_space=pl.ANY)] * 2
        read = len(operands) - 2

        def kernel(*refs):
            finish_kernel(*refs[:read], *refs[read + 2 :])

    shape = jax.ShapeDtypeStruct(gate_act.shape, jnp.bfloat16)
    return pl.pallas_call(
        kernel,
        grid=(width // block,),
        in_specs=specs,
        out_specs=[outer, outer],
        out_shape=[shape, shape],
        input_output_aliases=aliases,
        compiler_params=pltpu.CompilerParams(vmem_limit_bytes=32 * 1024 * 1024),
    )(*operands)


def on_device(grad_out, gate_act, up_act, down_weight):
    rows, cols = lax.axis_size("row"), lax.axis_size("col")
    steps = rows.bit_length() - 1
    tokens = grad_out.shape[0]
    pairs = [exchange_pairs(rows, cols, step) for step in range(steps)]

    def after(value, *others):
        return lax.optimization_barrier((value, *others))[0]

    def activation(gate, up):
        gate = gate.astype(jnp.float32)
        return (gate * jax.nn.sigmoid(gate) * up.astype(jnp.float32)).astype(jnp.bfloat16)

    hidden = activation(gate_act, up_act)
    hidden_came = lax.ppermute(hidden, BOTH, pairs[0])
    pieces = spread_tokens(grad_out, hidden, hidden_came, rows, cols)
    gathered = [hidden, hidden_came]
    for step in range(1, steps - 1):
        gathered = gathered + [lax.ppermute(part, BOTH, pairs[step]) for part in gathered]

    front, back = jnp.split(after(hidden, *pieces), [tokens * 3 // 4])
    front_came = lax.ppermute(front, BOTH, pairs[-1])
    back_came = lax.ppermute(back, BOTH, pairs[-1])
    gathered.append(jnp.concatenate([front_came, back_came]))

    blocks = gather_tokens(pieces)
    width = down_weight.shape[0]

    def product(block, start, stop, *before):
        return lax.dot_general(
            after(block, *before),
            down_weight[start:stop],
            (((1,), (1,)), ((), ())),
            preferred_element_type=jnp.float32,
        )

    def send(total, step):
        return lax.ppermute(total, BOTH, pairs[step])

    unit = width // 7
    total = [
        product(blocks[-1], 0, 3 * unit, front_came).astype(jnp.bfloat16),
        product(blocks[-1], 3 * unit, width, front_came).astype(jnp.bfloat16),
    ]
    tails = []
    for part in gathered[1 : rows // 2]:
        fore, rear = jnp.split(part, 2)
        fore = send(after(fore, total[0], back_came), steps - 1)
        rear = send(after(rear, total[1], back_came), steps - 1)
        gathered.append(jnp.concatenate([fore, rear]))
        tails += [fore, rear]
    total = after(jnp.concatenate(total, axis=1), *tails)

    blocks[:-1] = lax.optimization_barrier((*blocks[:-1], total))[:-1]
    turn = lax.axis_index("col") % steps
    grads = [
        lax.select_n(turn, *(blocks[row_offset(rows, place, t)] for t in range(steps)))
        if 0 < place < rows - 1
        else blocks[place]
        for place in range(rows)
    ]

    came = [[] for _ in range(rows)]
    came[rows - 2].append(send(total, 0))
    for step in range(steps - 1):
        for place in reversed(range(rows - 1)):
            if place & ((1 << step) - 1) or not place >> step & 1:
                continue
            total = product(grads[place], 0, width, total)
            for block in came[place]:
                total = total + block.astype(jnp.float32)
            total = total.astype(jnp.bfloat16)
            came[place ^ (1 << step)].append(send(total, step))

    starts, stops = [0, 3 * unit, 6 * unit], [3 * unit, 6 * unit, width]
    last = []
    for start, stop in zip(starts, stops):
        total = product(grads[rows // 2], start, stop, total)
        for block in came[rows // 2]:
            total = total + block[:, start:stop].astype(jnp.float32)
        total = total.astype(jnp.bfloat16)
        last.append(send(total, steps - 1))
    own = []
    for start, stop in zip(starts, stops):
        total = product(grads[0], start, stop, total)
        own.append(total)

    gathered, grads, own = lax.optimization_barrier((gathered, grads, own))
    grad_weight = lax.dot_general(
        jnp.concatenate(gathered, axis=0),
        jnp.concatenate(grads, axis=0),
        (((0,), (0,)), ((), ())),
        preferred_element_type=jnp.float32,
    )
    own, grad_weight = lax.optimization_barrier((own, grad_weight))

    gate_act, up_act = after(gate_act, hidden_came), after(up_act, hidden_came)
    outs = []
    for chunk, start in enumerate(starts):
        outs = finish(
            own[chunk], last[chunk], came[0], gate_act, up_act, outs, start, math.gcd(unit, 256)
        )
    return (*outs, grad_weight)


def solution(mesh):
    placed = (P("row", "col"), P("row", "col"), P("row", "col"), P("col", "row"))
    return jax.shard_map(
        on_device,
        mesh=mesh,
        in_specs=placed,
        out_specs=(P("row", "col"), P("row", "col"), P("col", "row")),
        check_vma=False,
    )
```

```python
import math

import jax
import jax.numpy as jnp
from jax import lax
from jax.experimental import pallas as pl
from jax.experimental.pallas import tpu as pltpu
from jax.sharding import PartitionSpec as P

BOTH = ("row", "col")


def exchange_pairs(rows, cols, step):
    bits = rows.bit_length() - 1
    return [
        (r * cols + c, (r ^ (1 << ((step + c) % bits))) * cols + c)
        for r in range(rows)
        for c in range(cols)
    ]


def row_offset(rows, place, turn):
    bits = rows.bit_length() - 1
    return sum(1 << ((step + turn) % bits) for step in range(bits) if place >> step & 1)


def spread_tokens(grad_out, hidden, hidden_came, rows, cols):
    share = cols // rows
    part = grad_out.shape[0] // cols
    row, col = lax.axis_index("row"), lax.axis_index("col")
    plane, lane = col // share, col % share

    pieces = grad_out.reshape(rows, share, part, grad_out.shape[1])
    arrived = []
    for shift in range(share):
        piece = lax.dynamic_index_in_dim(pieces, (lane + shift) % share, 1, keepdims=False)
        if shift:
            pairs = [
                (p * share + k, p * share + (k + shift) % share)
                for p in range(rows)
                for k in range(share)
            ]
            piece = lax.ppermute(piece, "col", pairs)
        arrived.append(piece)
    arrived = jnp.stack(arrived)
    mine = jnp.concatenate(
        [
            lax.dynamic_index_in_dim(arrived, (lane - k) % share, 0, keepdims=False)
            for k in range(share)
        ],
        axis=2,
    )

    mine, _ = lax.optimization_barrier((mine, hidden))

    held = []
    for flip in range(rows):
        piece = lax.dynamic_index_in_dim(mine, plane ^ flip, 0, keepdims=False)
        if flip:
            pairs = [(c, (c // share ^ flip) * share + c % share) for c in range(cols)]
            piece = lax.ppermute(piece, "col", pairs)
        held.append(piece)
    held, _ = lax.optimization_barrier((jnp.stack(held), hidden_came))

    blocks = [None] * rows
    for flip in reversed(range(rows)):
        piece = lax.dynamic_index_in_dim(held, row ^ flip ^ plane, 0, keepdims=False)
        if flip < rows - 1:
            piece, _ = lax.optimization_barrier((piece, blocks[-1]))
        if flip:
            piece = lax.ppermute(piece, "row", [(r, r ^ flip) for r in range(rows)])
        blocks[flip] = piece
    return blocks


def gather_tokens(blocks):
    first = lax.all_gather(blocks[-1], "col", axis=0, tiled=True)
    rest = lax.all_gather(jnp.stack(blocks[:-1]), "col", axis=1, tiled=True)
    return [rest[flip] for flip in range(len(blocks) - 1)] + [first]


def finish_kernel(own_ref, *refs):
    *came_refs, gate_ref, up_ref = refs[: len(refs) - 2]
    gate_out_ref, up_out_ref = refs[-2:]
    grad_hidden = own_ref[...]
    for came_ref in came_refs:
        grad_hidden = grad_hidden + came_ref[...].astype(jnp.float32)
    gate_value = gate_ref[...].astype(jnp.float32)
    up_value = up_ref[...].astype(jnp.float32)
    sigmoid_gate = 0.5 + 0.5 * jnp.tanh(0.5 * gate_value)
    gate_out_ref[...] = (
        grad_hidden * up_value * sigmoid_gate * (1.0 + gate_value * (1.0 - sigmoid_gate))
    ).astype(jnp.bfloat16)
    up_out_ref[...] = (grad_hidden * (gate_value * sigmoid_gate)).astype(jnp.bfloat16)


def finish(own, came, gate_act, up_act, outs, start, block):
    tokens, width = own.shape
    inner = pl.BlockSpec((tokens, block), lambda i: (0, i))
    outer = pl.BlockSpec((tokens, block), lambda i: (0, start // block + i))
    operands = [own, *came, gate_act, up_act]
    specs = [inner] * (1 + len(came)) + [outer] * 2
    kernel, aliases = finish_kernel, {}
    if outs:
        aliases = {len(operands): 0, len(operands) + 1: 1}
        operands += outs
        specs += [pl.BlockSpec(memory_space=pl.ANY)] * 2
        read = len(operands) - 2

        def kernel(*refs):
            finish_kernel(*refs[:read], *refs[read + 2 :])

    shape = jax.ShapeDtypeStruct(gate_act.shape, jnp.bfloat16)
    return pl.pallas_call(
        kernel,
        grid=(width // block,),
        in_specs=specs,
        out_specs=[outer, outer],
        out_shape=[shape, shape],
        input_output_aliases=aliases,
        compiler_params=pltpu.CompilerParams(vmem_limit_bytes=32 * 1024 * 1024),
    )(*operands)


def on_device(grad_out, gate_act, up_act, down_weight):
    rows, cols = lax.axis_size("row"), lax.axis_size("col")
    steps = rows.bit_length() - 1
    tokens = grad_out.shape[0]
    pairs = [exchange_pairs(rows, cols, step) for step in range(steps)]

    def after(value, *others):
        return lax.optimization_barrier((value, *others))[0]

    def activation(gate, up):
        gate = gate.astype(jnp.float32)
        return (gate * jax.nn.sigmoid(gate) * up.astype(jnp.float32)).astype(jnp.bfloat16)

    hidden = activation(gate_act, up_act)
    hidden_came = lax.ppermute(hidden, BOTH, pairs[0])
    pieces = spread_tokens(grad_out, hidden, hidden_came, rows, cols)
    gathered = [hidden, hidden_came]
    for step in range(1, steps - 1):
        gathered = gathered + [lax.ppermute(part, BOTH, pairs[step]) for part in gathered]

    front, back = jnp.split(hidden, 2)
    front_came = lax.ppermute(after(front, pieces[-1]), BOTH, pairs[-1])
    back_came = lax.ppermute(after(back, *pieces), BOTH, pairs[-1])
    gathered.append(jnp.concatenate([front_came, back_came]))

    blocks = gather_tokens(pieces)
    width = down_weight.shape[0]

    def product(block, start, stop, *before):
        return lax.dot_general(
            after(block, *before),
            down_weight[start:stop],
            (((1,), (1,)), ((), ())),
            preferred_element_type=jnp.float32,
        )

    def send(total, step):
        return lax.ppermute(total, BOTH, pairs[step])

    unit = width // 7
    total = product(blocks[-1], 0, 3 * unit, front_came).astype(jnp.bfloat16)
    rest = product(blocks[-1], 3 * unit, width, total).astype(jnp.bfloat16)
    total = jnp.concatenate([total, rest], axis=1)
    for part in gathered[1 : rows // 2]:
        gathered.append(send(after(part, rest, back_came), steps - 1))
    total = after(total, *gathered[rows // 2 + 1 :])

    blocks[:-1] = lax.optimization_barrier((*blocks[:-1], total))[:-1]
    turn = lax.axis_index("col") % steps
    grads = [
        lax.select_n(turn, *(blocks[row_offset(rows, place, t)] for t in range(steps)))
        if 0 < place < rows - 1
        else blocks[place]
        for place in range(rows)
    ]

    starts, stops = [0, 3 * unit, 6 * unit], [3 * unit, 6 * unit, width]
    chunks = range(len(starts))
    came = [[[] for _ in chunks] for _ in range(rows)]
    whole = send(total, 0)
    for chunk in chunks:
        came[rows - 2][chunk].append(whole[:, starts[chunk] : stops[chunk]])

    def message(place, chunk, *before):
        total = product(grads[place], starts[chunk], stops[chunk], *before)
        for block in came[place][chunk]:
            total = total + block.astype(jnp.float32)
        return total.astype(jnp.bfloat16)

    def own_product(chunk, *before):
        return product(grads[0], starts[chunk], stops[chunk], *before)

    for step in range(steps - 1):
        for place in reversed(range(rows - 1)):
            if place & ((1 << step) - 1) or not place >> step & 1:
                continue
            for chunk in chunks:
                total = message(place, chunk, total)
                came[place ^ (1 << step)][chunk].append(send(total, step))
    own = [own_product(0, total)]
    own.append(own_product(1, own[0]))
    total = message(rows // 2, 0, own[1])
    last = [send(total, steps - 1)]

    gathered, grads, _ = lax.optimization_barrier((gathered, grads, total))
    grad_weight = lax.dot_general(
        jnp.concatenate(gathered, axis=0),
        jnp.concatenate(grads, axis=0),
        (((0,), (0,)), ((), ())),
        preferred_element_type=jnp.float32,
    )
    total = after(message(rows // 2, 1, grad_weight), last[0], *sum(came[0], []))
    last.append(send(total, steps - 1))
    total = message(rows // 2, 2, total)
    last.append(send(total, steps - 1))
    own.append(own_product(2, total))

    gate_act, up_act = after(gate_act, hidden_came), after(up_act, hidden_came)
    outs = []
    for chunk, start in enumerate(starts):
        outs = finish(
            own[chunk],
            [after(block, grad_weight) for block in (*came[0][chunk], last[chunk])],
            gate_act,
            up_act,
            outs,
            start,
            math.gcd(unit, 256),
        )
    return (*outs, grad_weight)


def solution(mesh):
    placed = (P("row", "col"), P("row", "col"), P("row", "col"), P("col", "row"))
    return jax.shard_map(
        on_device,
        mesh=mesh,
        in_specs=placed,
        out_specs=(P("row", "col"), P("row", "col"), P("col", "row")),
        check_vma=False,
    )
```

```python
import math

import jax
import jax.numpy as jnp
from jax import lax
from jax.experimental import pallas as pl
from jax.experimental.pallas import tpu as pltpu
from jax.sharding import PartitionSpec as P

BOTH = ("row", "col")


def exchange_pairs(rows, cols, step):
    bits = rows.bit_length() - 1
    return [
        (r * cols + c, (r ^ (1 << ((step + c) % bits))) * cols + c)
        for r in range(rows)
        for c in range(cols)
    ]


def row_offset(rows, place, turn):
    bits = rows.bit_length() - 1
    return sum(1 << ((step + turn) % bits) for step in range(bits) if place >> step & 1)


def spread_tokens(grad_out, hidden, hidden_came, rows, cols):
    share = cols // rows
    part = grad_out.shape[0] // cols
    row, col = lax.axis_index("row"), lax.axis_index("col")
    plane, lane = col // share, col % share

    pieces = grad_out.reshape(rows, share, part, grad_out.shape[1])
    arrived = []
    for shift in range(share):
        piece = lax.dynamic_index_in_dim(pieces, (lane + shift) % share, 1, keepdims=False)
        if shift:
            pairs = [
                (p * share + k, p * share + (k + shift) % share)
                for p in range(rows)
                for k in range(share)
            ]
            piece = lax.ppermute(piece, "col", pairs)
        arrived.append(piece)
    arrived = jnp.stack(arrived)
    mine = jnp.concatenate(
        [
            lax.dynamic_index_in_dim(arrived, (lane - k) % share, 0, keepdims=False)
            for k in range(share)
        ],
        axis=2,
    )

    mine, _ = lax.optimization_barrier((mine, hidden))

    held = []
    for flip in range(rows):
        piece = lax.dynamic_index_in_dim(mine, plane ^ flip, 0, keepdims=False)
        if flip:
            pairs = [(c, (c // share ^ flip) * share + c % share) for c in range(cols)]
            piece = lax.ppermute(piece, "col", pairs)
        held.append(piece)
    held, _ = lax.optimization_barrier((jnp.stack(held), hidden_came))

    blocks = [None] * rows
    for flip in reversed(range(rows)):
        piece = lax.dynamic_index_in_dim(held, row ^ flip ^ plane, 0, keepdims=False)
        if flip:
            piece = lax.ppermute(piece, "row", [(r, r ^ flip) for r in range(rows)])
        blocks[flip] = piece
    return blocks


def gather_tokens(blocks, before):
    first = lax.all_gather(blocks[-1], "col", axis=0, tiled=True)
    rest, _ = lax.optimization_barrier((jnp.stack(blocks[:-1]), before))
    rest = lax.all_gather(rest, "col", axis=1, tiled=True)
    return [rest[flip] for flip in range(len(blocks) - 1)] + [first]


def finish_kernel(own_ref, *refs):
    *came_refs, gate_ref, up_ref = refs[: len(refs) - 2]
    gate_out_ref, up_out_ref = refs[-2:]
    grad_hidden = own_ref[...]
    for came_ref in came_refs:
        grad_hidden = grad_hidden + came_ref[...].astype(jnp.float32)
    gate_value = gate_ref[...].astype(jnp.float32)
    up_value = up_ref[...].astype(jnp.float32)
    sigmoid_gate = 0.5 + 0.5 * jnp.tanh(0.5 * gate_value)
    gate_out_ref[...] = (
        grad_hidden * up_value * sigmoid_gate * (1.0 + gate_value * (1.0 - sigmoid_gate))
    ).astype(jnp.bfloat16)
    up_out_ref[...] = (grad_hidden * (gate_value * sigmoid_gate)).astype(jnp.bfloat16)


def finish(own, came, gate_act, up_act, outs, start, block):
    tokens, width = own.shape
    inner = pl.BlockSpec((tokens, block), lambda i: (0, i))
    outer = pl.BlockSpec((tokens, block), lambda i: (0, start // block + i))
    operands = [own, *came, gate_act, up_act]
    specs = [inner] * (1 + len(came)) + [outer] * 2
    kernel, aliases = finish_kernel, {}
    if outs:
        aliases = {len(operands): 0, len(operands) + 1: 1}
        operands += outs
        specs += [pl.BlockSpec(memory_space=pl.ANY)] * 2
        read = len(operands) - 2

        def kernel(*refs):
            finish_kernel(*refs[:read], *refs[read + 2 :])

    shape = jax.ShapeDtypeStruct(gate_act.shape, jnp.bfloat16)
    return pl.pallas_call(
        kernel,
        grid=(width // block,),
        in_specs=specs,
        out_specs=[outer, outer],
        out_shape=[shape, shape],
        input_output_aliases=aliases,
        compiler_params=pltpu.CompilerParams(vmem_limit_bytes=32 * 1024 * 1024),
    )(*operands)


def on_device(grad_out, gate_act, up_act, down_weight):
    rows, cols = lax.axis_size("row"), lax.axis_size("col")
    steps = rows.bit_length() - 1
    tokens = grad_out.shape[0]
    pairs = [exchange_pairs(rows, cols, step) for step in range(steps)]

    def after(value, *others):
        return lax.optimization_barrier((value, *others))[0]

    def activation(gate, up):
        gate = gate.astype(jnp.float32)
        return (gate * jax.nn.sigmoid(gate) * up.astype(jnp.float32)).astype(jnp.bfloat16)

    hidden = activation(gate_act, up_act)
    hidden_came = lax.ppermute(hidden, BOTH, pairs[0])
    pieces = spread_tokens(grad_out, hidden, hidden_came, rows, cols)
    gathered = [hidden, hidden_came]
    for step in range(1, steps - 1):
        gathered = gathered + [lax.ppermute(part, BOTH, pairs[step]) for part in gathered]

    front, back = jnp.split(hidden, 2)
    front_came = lax.ppermute(after(front, pieces[-1]), BOTH, pairs[-1])
    back_came = lax.ppermute(after(back, *pieces), BOTH, pairs[-1])
    gathered.append(jnp.concatenate([front_came, back_came]))

    blocks = gather_tokens(pieces, front_came)
    width = down_weight.shape[0]

    def product(block, start, stop, *before):
        return lax.dot_general(
            after(block, *before),
            down_weight[start:stop],
            (((1,), (1,)), ((), ())),
            preferred_element_type=jnp.float32,
        )

    def send(total, step):
        return lax.ppermute(total, BOTH, pairs[step])

    unit = width // 7
    total = product(blocks[-1], 0, 3 * unit, front_came).astype(jnp.bfloat16)
    for part in gathered[1 : rows // 2]:
        gathered.append(send(after(part, total, back_came), steps - 1))
    rest = product(blocks[-1], 3 * unit, width, total).astype(jnp.bfloat16)
    total = jnp.concatenate([total, rest], axis=1)
    total = after(total, *gathered[rows // 2 + 1 :])

    blocks[:-1] = lax.optimization_barrier((*blocks[:-1], total))[:-1]
    turn = lax.axis_index("col") % steps
    grads = [
        lax.select_n(turn, *(blocks[row_offset(rows, place, t)] for t in range(steps)))
        if 0 < place < rows - 1
        else blocks[place]
        for place in range(rows)
    ]

    starts, stops = [0, 3 * unit, 6 * unit], [3 * unit, 6 * unit, width]
    chunks = range(len(starts))
    came = [[[] for _ in chunks] for _ in range(rows)]
    whole = send(total, 0)
    for chunk in chunks:
        came[rows - 2][chunk].append(whole[:, starts[chunk] : stops[chunk]])

    def message(place, chunk, *before):
        total = product(grads[place], starts[chunk], stops[chunk], *before)
        for block in came[place][chunk]:
            total = total + block.astype(jnp.float32)
        return total.astype(jnp.bfloat16)

    def own_product(chunk, *before):
        return product(grads[0], starts[chunk], stops[chunk], *before)

    for step in range(steps - 1):
        for place in reversed(range(rows - 1)):
            if place & ((1 << step) - 1) or not place >> step & 1:
                continue
            for chunk in chunks:
                total = message(place, chunk, total)
                came[place ^ (1 << step)][chunk].append(send(total, step))
    own = [own_product(0, total)]
    own.append(own_product(1, own[0]))
    total = message(rows // 2, 0, own[1])
    last = [send(total, steps - 1)]

    gathered, grads, _ = lax.optimization_barrier((gathered, grads, total))
    grad_weight = lax.dot_general(
        jnp.concatenate(gathered, axis=0),
        jnp.concatenate(grads, axis=0),
        (((0,), (0,)), ((), ())),
        preferred_element_type=jnp.float32,
    )
    total = after(message(rows // 2, 1, grad_weight), last[0], *sum(came[0], []))
    last.append(send(total, steps - 1))
    total = message(rows // 2, 2, total)
    last.append(send(total, steps - 1))
    own.append(own_product(2, total))

    gate_act, up_act = after(gate_act, hidden_came), after(up_act, hidden_came)
    outs = []
    for chunk, start in enumerate(starts):
        outs = finish(
            own[chunk],
            [after(block, grad_weight, *outs) for block in (*came[0][chunk], last[chunk])],
            gate_act,
            up_act,
            outs,
            start,
            math.gcd(unit, 256),
        )
    return (*outs, grad_weight)


def solution(mesh):
    placed = (P("row", "col"), P("row", "col"), P("row", "col"), P("col", "row"))
    return jax.shard_map(
        on_device,
        mesh=mesh,
        in_specs=placed,
        out_specs=(P("row", "col"), P("row", "col"), P("col", "row")),
        check_vma=False,
    )
```

```python
import math

import jax
import jax.numpy as jnp
from jax import lax
from jax.experimental import pallas as pl
from jax.experimental.pallas import tpu as pltpu
from jax.sharding import PartitionSpec as P

BOTH = ("row", "col")


def exchange_pairs(rows, cols, step):
    bits = rows.bit_length() - 1
    return [
        (r * cols + c, (r ^ (1 << ((step + c) % bits))) * cols + c)
        for r in range(rows)
        for c in range(cols)
    ]


def row_offset(rows, place, turn):
    bits = rows.bit_length() - 1
    return sum(1 << ((step + turn) % bits) for step in range(bits) if place >> step & 1)


def spread_tokens(grad_out, hidden, hidden_came, rows, cols):
    share = cols // rows
    part = grad_out.shape[0] // cols
    row, col = lax.axis_index("row"), lax.axis_index("col")
    plane, lane = col // share, col % share

    pieces = grad_out.reshape(rows, share, part, grad_out.shape[1])
    arrived = []
    for shift in range(share):
        piece = lax.dynamic_index_in_dim(pieces, (lane + shift) % share, 1, keepdims=False)
        if shift:
            pairs = [
                (p * share + k, p * share + (k + shift) % share)
                for p in range(rows)
                for k in range(share)
            ]
            piece = lax.ppermute(piece, "col", pairs)
        arrived.append(piece)
    arrived = jnp.stack(arrived)
    mine = jnp.concatenate(
        [
            lax.dynamic_index_in_dim(arrived, (lane - k) % share, 0, keepdims=False)
            for k in range(share)
        ],
        axis=2,
    )

    mine, _ = lax.optimization_barrier((mine, hidden))

    held = []
    for flip in range(rows):
        piece = lax.dynamic_index_in_dim(mine, plane ^ flip, 0, keepdims=False)
        if flip:
            pairs = [(c, (c // share ^ flip) * share + c % share) for c in range(cols)]
            piece = lax.ppermute(piece, "col", pairs)
        held.append(piece)
    held = jnp.stack(held)

    blocks = [None] * rows
    for flip in reversed(range(rows)):
        piece = lax.dynamic_index_in_dim(held, row ^ flip ^ plane, 0, keepdims=False)
        if flip < rows - 1:
            piece = lax.optimization_barrier((piece, blocks[-1]))[0]
        if flip:
            piece = lax.ppermute(piece, "row", [(r, r ^ flip) for r in range(rows)])
        if flip == rows - 1:
            piece = lax.optimization_barrier((piece, hidden_came))[0]
        blocks[flip] = piece
    return blocks


def gather_tokens(blocks):
    first = lax.all_gather(blocks[-1], "col", axis=0, tiled=True)
    rest = lax.all_gather(jnp.stack(blocks[:-1]), "col", axis=1, tiled=True)
    return [rest[flip] for flip in range(len(blocks) - 1)] + [first]


def finish_kernel(own_ref, *refs):
    *came_refs, gate_ref, up_ref = refs[: len(refs) - 2]
    gate_out_ref, up_out_ref = refs[-2:]
    grad_hidden = own_ref[...]
    for came_ref in came_refs:
        grad_hidden = grad_hidden + came_ref[...].astype(jnp.float32)
    gate_value = gate_ref[...].astype(jnp.float32)
    up_value = up_ref[...].astype(jnp.float32)
    sigmoid_gate = 0.5 + 0.5 * jnp.tanh(0.5 * gate_value)
    gate_out_ref[...] = (
        grad_hidden * up_value * sigmoid_gate * (1.0 + gate_value * (1.0 - sigmoid_gate))
    ).astype(jnp.bfloat16)
    up_out_ref[...] = (grad_hidden * (gate_value * sigmoid_gate)).astype(jnp.bfloat16)


def finish(own, came, gate_act, up_act, outs, start, block):
    tokens, width = own.shape
    inner = pl.BlockSpec((tokens, block), lambda i: (0, i))
    outer = pl.BlockSpec((tokens, block), lambda i: (0, start // block + i))
    operands = [own, *came, gate_act, up_act]
    specs = [inner] * (1 + len(came)) + [outer] * 2
    kernel, aliases = finish_kernel, {}
    if outs:
        aliases = {len(operands): 0, len(operands) + 1: 1}
        operands += outs
        specs += [pl.BlockSpec(memory_space=pl.ANY)] * 2
        read = len(operands) - 2

        def kernel(*refs):
            finish_kernel(*refs[:read], *refs[read + 2 :])

    shape = jax.ShapeDtypeStruct(gate_act.shape, jnp.bfloat16)
    return pl.pallas_call(
        kernel,
        grid=(width // block,),
        in_specs=specs,
        out_specs=[outer, outer],
        out_shape=[shape, shape],
        input_output_aliases=aliases,
        compiler_params=pltpu.CompilerParams(vmem_limit_bytes=32 * 1024 * 1024),
    )(*operands)


def on_device(grad_out, gate_act, up_act, down_weight):
    rows, cols = lax.axis_size("row"), lax.axis_size("col")
    steps = rows.bit_length() - 1
    tokens = grad_out.shape[0]
    pairs = [exchange_pairs(rows, cols, step) for step in range(steps)]

    def after(value, *others):
        return lax.optimization_barrier((value, *others))[0]

    def activation(gate, up):
        gate = gate.astype(jnp.float32)
        return (gate * jax.nn.sigmoid(gate) * up.astype(jnp.float32)).astype(jnp.bfloat16)

    hidden = activation(gate_act, up_act)
    hidden_came = lax.ppermute(hidden, BOTH, pairs[0])
    pieces = spread_tokens(grad_out, hidden, hidden_came, rows, cols)
    gathered = [hidden, hidden_came]
    for step in range(1, steps - 1):
        gathered = gathered + [lax.ppermute(part, BOTH, pairs[step]) for part in gathered]

    gathered.append(lax.ppermute(after(hidden, *pieces), BOTH, pairs[-1]))

    blocks = gather_tokens(pieces)
    width = down_weight.shape[0]

    def product(block, start, stop, *before):
        return lax.dot_general(
            after(block, *before),
            down_weight[start:stop],
            (((1,), (1,)), ((), ())),
            preferred_element_type=jnp.float32,
        )

    def send(total, step):
        return lax.ppermute(total, BOTH, pairs[step])

    unit = width // 7
    total = product(blocks[-1], 0, 3 * unit).astype(jnp.bfloat16)
    for part in gathered[1 : rows // 2]:
        gathered.append(send(after(part, total), steps - 1))
    rest = product(blocks[-1], 3 * unit, width, total, gathered[rows // 2]).astype(jnp.bfloat16)
    total = jnp.concatenate([total, rest], axis=1)
    total = after(total, *gathered[rows // 2 + 1 :])

    blocks[:-1] = lax.optimization_barrier((*blocks[:-1], total))[:-1]
    turn = lax.axis_index("col") % steps
    grads = [
        lax.select_n(turn, *(blocks[row_offset(rows, place, t)] for t in range(steps)))
        if 0 < place < rows - 1
        else blocks[place]
        for place in range(rows)
    ]

    starts, stops = [0, 3 * unit, 6 * unit], [3 * unit, 6 * unit, width]
    chunks = range(len(starts))
    came = [[[] for _ in chunks] for _ in range(rows)]
    whole = send(total, 0)
    for chunk in chunks:
        came[rows - 2][chunk].append(whole[:, starts[chunk] : stops[chunk]])

    def message(place, chunk, *before):
        total = product(grads[place], starts[chunk], stops[chunk], *before)
        for block in came[place][chunk]:
            total = total + block.astype(jnp.float32)
        return total.astype(jnp.bfloat16)

    def own_product(chunk, *before):
        return product(grads[0], starts[chunk], stops[chunk], *before)

    for step in range(steps - 1):
        for place in reversed(range(rows - 1)):
            if place & ((1 << step) - 1) or not place >> step & 1:
                continue
            for chunk in chunks:
                total = message(place, chunk, total)
                came[place ^ (1 << step)][chunk].append(send(total, step))
    own = [own_product(0, total)]
    own.append(own_product(1, own[0]))
    total = message(rows // 2, 0, own[1])
    last = [send(total, steps - 1)]

    gathered, grads, _ = lax.optimization_barrier((gathered, grads, total))
    grad_weight = lax.dot_general(
        jnp.concatenate(gathered, axis=0),
        jnp.concatenate(grads, axis=0),
        (((0,), (0,)), ((), ())),
        preferred_element_type=jnp.float32,
    )

    total = after(message(rows // 2, 1, grad_weight), *sum(came[0], []))
    last.append(send(total, steps - 1))
    total = after(message(rows // 2, 2, total), last[0])
    last.append(send(total, steps - 1))
    own.append(own_product(2, total))

    gate_act, up_act = after(gate_act, hidden_came), after(up_act, hidden_came)
    outs = []
    for chunk, start in enumerate(starts):
        outs = finish(
            own[chunk],
            [after(block, grad_weight, *outs) for block in (*came[0][chunk], last[chunk])],
            gate_act,
            up_act,
            outs,
            start,
            math.gcd(unit, 256),
        )
    return (*outs, grad_weight)


def solution(mesh):
    placed = (P("row", "col"), P("row", "col"), P("row", "col"), P("col", "row"))
    return jax.shard_map(
        on_device,
        mesh=mesh,
        in_specs=placed,
        out_specs=(P("row", "col"), P("row", "col"), P("col", "row")),
        check_vma=False,
    )
```

```python
import math

import jax
import jax.numpy as jnp
from jax import lax
from jax.experimental import pallas as pl
from jax.experimental.pallas import tpu as pltpu
from jax.sharding import PartitionSpec as P

BOTH = ("row", "col")


def exchange_pairs(rows, cols, step):
    bits = rows.bit_length() - 1
    return [
        (r * cols + c, (r ^ (1 << ((step + c) % bits))) * cols + c)
        for r in range(rows)
        for c in range(cols)
    ]


def row_offset(rows, place, turn):
    bits = rows.bit_length() - 1
    return sum(1 << ((step + turn) % bits) for step in range(bits) if place >> step & 1)


def spread_tokens(grad_out, hidden, hidden_came, rows, cols):
    share = cols // rows
    part = grad_out.shape[0] // cols
    row, col = lax.axis_index("row"), lax.axis_index("col")
    plane, lane = col // share, col % share

    pieces = grad_out.reshape(rows, share, part, grad_out.shape[1])
    arrived = []
    for shift in range(share):
        piece = lax.dynamic_index_in_dim(pieces, (lane + shift) % share, 1, keepdims=False)
        if shift:
            pairs = [
                (p * share + k, p * share + (k + shift) % share)
                for p in range(rows)
                for k in range(share)
            ]
            piece = lax.ppermute(piece, "col", pairs)
        arrived.append(piece)
    arrived = jnp.stack(arrived)
    mine = jnp.concatenate(
        [
            lax.dynamic_index_in_dim(arrived, (lane - k) % share, 0, keepdims=False)
            for k in range(share)
        ],
        axis=2,
    )

    mine, _ = lax.optimization_barrier((mine, hidden))

    held = []
    for flip in range(rows):
        piece = lax.dynamic_index_in_dim(mine, plane ^ flip, 0, keepdims=False)
        if flip:
            pairs = [(c, (c // share ^ flip) * share + c % share) for c in range(cols)]
            piece = lax.ppermute(piece, "col", pairs)
        held.append(piece)
    held = jnp.stack(held)

    blocks = [None] * rows
    for flip in reversed(range(rows)):
        piece = lax.dynamic_index_in_dim(held, row ^ flip ^ plane, 0, keepdims=False)
        if flip:
            piece = lax.ppermute(piece, "row", [(r, r ^ flip) for r in range(rows)])
        blocks[flip] = piece
    blocks[-1] = lax.optimization_barrier((blocks[-1], *blocks[1:-1], *hidden_came))[0]
    return blocks


def finish_kernel(own_ref, *refs):
    *came_refs, gate_ref, up_ref = refs[: len(refs) - 2]
    gate_out_ref, up_out_ref = refs[-2:]
    grad_hidden = own_ref[...]
    for came_ref in came_refs:
        grad_hidden = grad_hidden + came_ref[...].astype(jnp.float32)
    gate_value = gate_ref[...].astype(jnp.float32)
    up_value = up_ref[...].astype(jnp.float32)
    sigmoid_gate = 0.5 + 0.5 * jnp.tanh(0.5 * gate_value)
    gate_out_ref[...] = (
        grad_hidden * up_value * sigmoid_gate * (1.0 + gate_value * (1.0 - sigmoid_gate))
    ).astype(jnp.bfloat16)
    up_out_ref[...] = (grad_hidden * (gate_value * sigmoid_gate)).astype(jnp.bfloat16)


def finish(own, came, gate_act, up_act, outs, start, block):
    tokens, width = own.shape
    inner = pl.BlockSpec((tokens, block), lambda i: (0, i))
    outer = pl.BlockSpec((tokens, block), lambda i: (0, start // block + i))
    operands = [own, *came, gate_act, up_act]
    specs = [inner] * (1 + len(came)) + [outer] * 2
    kernel, aliases = finish_kernel, {}
    if outs:
        aliases = {len(operands): 0, len(operands) + 1: 1}
        operands += outs
        specs += [pl.BlockSpec(memory_space=pl.ANY)] * 2
        read = len(operands) - 2

        def kernel(*refs):
            finish_kernel(*refs[:read], *refs[read + 2 :])

    shape = jax.ShapeDtypeStruct(gate_act.shape, jnp.bfloat16)
    return pl.pallas_call(
        kernel,
        grid=(width // block,),
        in_specs=specs,
        out_specs=[outer, outer],
        out_shape=[shape, shape],
        input_output_aliases=aliases,
        compiler_params=pltpu.CompilerParams(vmem_limit_bytes=32 * 1024 * 1024),
    )(*operands)


def on_device(grad_out, gate_act, up_act, down_weight):
    rows, cols = lax.axis_size("row"), lax.axis_size("col")
    steps = rows.bit_length() - 1
    tokens = grad_out.shape[0]
    pairs = [exchange_pairs(rows, cols, step) for step in range(steps)]

    def after(value, *others):
        return lax.optimization_barrier((value, *others))[0]

    def activation(gate, up):
        gate = gate.astype(jnp.float32)
        return (gate * jax.nn.sigmoid(gate) * up.astype(jnp.float32)).astype(jnp.bfloat16)

    gate_halves, up_halves = jnp.split(gate_act, 2), jnp.split(up_act, 2)
    front = activation(gate_halves[0], up_halves[0])
    back = activation(after(gate_halves[1], front), after(up_halves[1], front))
    hidden_came = [lax.ppermute(half, BOTH, pairs[0]) for half in (front, back)]
    pieces = spread_tokens(grad_out, back, hidden_came, rows, cols)
    hidden = jnp.concatenate([front, back])
    gathered = [hidden, jnp.concatenate(hidden_came)]
    for step in range(1, steps - 1):
        gathered = gathered + [lax.ppermute(part, BOTH, pairs[step]) for part in gathered]

    gathered.append(lax.ppermute(after(hidden, *pieces), BOTH, pairs[-1]))

    first = lax.all_gather(pieces[-1], "col", axis=0, tiled=True)
    others = lax.all_gather(after(jnp.stack(pieces[:-1]), first), "col", axis=1, tiled=True)
    width = down_weight.shape[0]

    def product(block, start, stop, *before):
        return lax.dot_general(
            after(block, *before),
            down_weight[start:stop],
            (((1,), (1,)), ((), ())),
            preferred_element_type=jnp.float32,
        )

    def send(total, step):
        return lax.ppermute(total, BOTH, pairs[step])

    unit = width // 7
    total = product(first, 0, 3 * unit).astype(jnp.bfloat16)
    for part in gathered[1 : rows // 2]:
        gathered.append(send(after(part, total), steps - 1))
    rest = product(first, 3 * unit, width, total, gathered[rows // 2]).astype(jnp.bfloat16)
    total = jnp.concatenate([total, rest], axis=1)
    total = after(total, *gathered[rows // 2 + 1 :])

    others = after(others, total)
    blocks = [*(others[flip] for flip in range(rows - 1)), first]
    turn = lax.axis_index("col") % steps
    grads = [
        lax.select_n(turn, *(blocks[row_offset(rows, place, t)] for t in range(steps)))
        if 0 < place < rows - 1
        else blocks[place]
        for place in range(rows)
    ]

    starts, stops = [0, 3 * unit, 6 * unit], [3 * unit, 6 * unit, width]
    chunks = range(len(starts))
    came = [[[] for _ in chunks] for _ in range(rows)]
    whole = send(total, 0)
    for chunk in chunks:
        came[rows - 2][chunk].append(whole[:, starts[chunk] : stops[chunk]])

    def message(place, chunk, *before):
        total = product(grads[place], starts[chunk], stops[chunk], *before)
        for block in came[place][chunk]:
            total = total + block.astype(jnp.float32)
        return total.astype(jnp.bfloat16)

    def own_product(chunk, *before):
        return product(grads[0], starts[chunk], stops[chunk], *before)

    for step in range(steps - 1):
        for place in reversed(range(rows - 1)):
            if place & ((1 << step) - 1) or not place >> step & 1:
                continue
            for chunk in chunks:
                total = message(place, chunk, total)
                came[place ^ (1 << step)][chunk].append(send(total, step))
    last = []
    for chunk in chunks[:-1]:
        total = message(rows // 2, chunk, total)
        last.append(send(total, steps - 1))
    own = []
    for chunk in chunks:
        total = own_product(chunk, total)
        own.append(total)

    gathered, grads, own = lax.optimization_barrier((gathered, grads, own))
    grad_weight = lax.dot_general(
        jnp.concatenate(gathered, axis=0),
        jnp.concatenate(grads, axis=0),
        (((0,), (0,)), ((), ())),
        preferred_element_type=jnp.float32,
    )

    total = message(rows // 2, len(last), grad_weight)
    last.append(send(after(total, last[0], *sum(came[0], [])), steps - 1))

    gate_act, up_act = after(gate_act, front), after(up_act, front)
    outs = []
    for chunk, start in enumerate(starts):
        outs = finish(
            own[chunk],
            [after(block, grad_weight, *outs) for block in (*came[0][chunk], last[chunk])],
            gate_act,
            up_act,
            outs,
            start,
            math.gcd(unit, 256),
        )
    return (*outs, grad_weight)


def solution(mesh):
    placed = (P("row", "col"), P("row", "col"), P("row", "col"), P("col", "row"))
    return jax.shard_map(
        on_device,
        mesh=mesh,
        in_specs=placed,
        out_specs=(P("row", "col"), P("row", "col"), P("col", "row")),
        check_vma=False,
    )
```

```python
import math

import jax
import jax.numpy as jnp
from jax import lax
from jax.experimental import pallas as pl
from jax.experimental.pallas import tpu as pltpu
from jax.sharding import PartitionSpec as P

BOTH = ("row", "col")


def exchange_pairs(rows, cols, step):
    bits = rows.bit_length() - 1
    return [
        (r * cols + c, (r ^ (1 << ((step + c) % bits))) * cols + c)
        for r in range(rows)
        for c in range(cols)
    ]


def row_offset(rows, place, turn):
    bits = rows.bit_length() - 1
    return sum(1 << ((step + turn) % bits) for step in range(bits) if place >> step & 1)


def spread_tokens(grad_out, hidden, hidden_came, rows, cols):
    share = cols // rows
    part = grad_out.shape[0] // cols
    row, col = lax.axis_index("row"), lax.axis_index("col")
    plane, lane = col // share, col % share

    pieces = grad_out.reshape(rows, share, part, grad_out.shape[1])
    arrived = []
    for shift in range(share):
        piece = lax.dynamic_index_in_dim(pieces, (lane + shift) % share, 1, keepdims=False)
        if shift:
            pairs = [
                (p * share + k, p * share + (k + shift) % share)
                for p in range(rows)
                for k in range(share)
            ]
            piece = lax.ppermute(piece, "col", pairs)
        arrived.append(piece)
    arrived = jnp.stack(arrived)
    mine = jnp.concatenate(
        [
            lax.dynamic_index_in_dim(arrived, (lane - k) % share, 0, keepdims=False)
            for k in range(share)
        ],
        axis=2,
    )

    mine, _ = lax.optimization_barrier((mine, hidden))

    held = []
    for flip in range(rows):
        piece = lax.dynamic_index_in_dim(mine, plane ^ flip, 0, keepdims=False)
        if flip:
            pairs = [(c, (c // share ^ flip) * share + c % share) for c in range(cols)]
            piece = lax.ppermute(piece, "col", pairs)
        held.append(piece)
    held = jnp.stack(held)

    blocks = [None] * rows
    for flip in reversed(range(rows)):
        piece = lax.dynamic_index_in_dim(held, row ^ flip ^ plane, 0, keepdims=False)
        if flip < rows - 1:
            piece = lax.optimization_barrier((piece, blocks[-1]))[0]
        if flip:
            piece = lax.ppermute(piece, "row", [(r, r ^ flip) for r in range(rows)])
        if flip == rows - 1:
            piece = lax.optimization_barrier((piece, hidden_came))[0]
        blocks[flip] = piece
    return blocks


def gather_tokens(blocks, before):
    first = lax.all_gather(blocks[-1], "col", axis=0, tiled=True)
    rest, _ = lax.optimization_barrier((jnp.stack(blocks[:-1]), before))
    rest = lax.all_gather(rest, "col", axis=1, tiled=True)
    return [rest[flip] for flip in range(len(blocks) - 1)] + [first]


def finish_kernel(own_ref, *refs):
    *came_refs, gate_ref, up_ref = refs[: len(refs) - 2]
    gate_out_ref, up_out_ref = refs[-2:]
    grad_hidden = own_ref[...]
    for came_ref in came_refs:
        grad_hidden = grad_hidden + came_ref[...].astype(jnp.float32)
    gate_value = gate_ref[...].astype(jnp.float32)
    up_value = up_ref[...].astype(jnp.float32)
    sigmoid_gate = 0.5 + 0.5 * jnp.tanh(0.5 * gate_value)
    gate_out_ref[...] = (
        grad_hidden * up_value * sigmoid_gate * (1.0 + gate_value * (1.0 - sigmoid_gate))
    ).astype(jnp.bfloat16)
    up_out_ref[...] = (grad_hidden * (gate_value * sigmoid_gate)).astype(jnp.bfloat16)


def finish(own, came, gate_act, up_act, outs, start, block):
    tokens, width = own.shape
    inner = pl.BlockSpec((tokens, block), lambda i: (0, i))
    outer = pl.BlockSpec((tokens, block), lambda i: (0, start // block + i))
    operands = [own, *came, gate_act, up_act]
    specs = [inner] * (1 + len(came)) + [outer] * 2
    kernel, aliases = finish_kernel, {}
    if outs:
        aliases = {len(operands): 0, len(operands) + 1: 1}
        operands += outs
        specs += [pl.BlockSpec(memory_space=pl.ANY)] * 2
        read = len(operands) - 2

        def kernel(*refs):
            finish_kernel(*refs[:read], *refs[read + 2 :])

    shape = jax.ShapeDtypeStruct(gate_act.shape, jnp.bfloat16)
    return pl.pallas_call(
        kernel,
        grid=(width // block,),
        in_specs=specs,
        out_specs=[outer, outer],
        out_shape=[shape, shape],
        input_output_aliases=aliases,
        compiler_params=pltpu.CompilerParams(vmem_limit_bytes=32 * 1024 * 1024),
    )(*operands)


def on_device(grad_out, gate_act, up_act, down_weight):
    rows, cols = lax.axis_size("row"), lax.axis_size("col")
    steps = rows.bit_length() - 1
    tokens = grad_out.shape[0]
    pairs = [exchange_pairs(rows, cols, step) for step in range(steps)]

    def after(value, *others):
        return lax.optimization_barrier((value, *others))[0]

    def activation(gate, up):
        gate = gate.astype(jnp.float32)
        return (gate * jax.nn.sigmoid(gate) * up.astype(jnp.float32)).astype(jnp.bfloat16)

    hidden = activation(gate_act, up_act)
    hidden_came = lax.ppermute(hidden, BOTH, pairs[0])
    pieces = spread_tokens(grad_out, hidden, hidden_came, rows, cols)
    gathered = [hidden, hidden_came]
    for step in range(1, steps - 1):
        gathered = gathered + [lax.ppermute(part, BOTH, pairs[step]) for part in gathered]

    little, large = jnp.split(hidden, [tokens // 8])
    little_came = lax.ppermute(after(little, pieces[-1]), BOTH, pairs[-1])
    large_came = lax.ppermute(after(large, *pieces, little_came), BOTH, pairs[-1])
    gathered.append(jnp.concatenate([little_came, large_came]))

    blocks = gather_tokens(pieces, little_came)
    width = down_weight.shape[0]

    def product(block, start, stop, *before):
        return lax.dot_general(
            after(block, *before),
            down_weight[start:stop],
            (((1,), (1,)), ((), ())),
            preferred_element_type=jnp.float32,
        )

    def send(total, step):
        return lax.ppermute(total, BOTH, pairs[step])

    unit = width // 7
    total = product(blocks[-1], 0, 3 * unit).astype(jnp.bfloat16)
    for part in gathered[1 : rows // 2]:
        gathered.append(send(after(part, total), steps - 1))
    rest = product(blocks[-1], 3 * unit, width, total, large_came).astype(jnp.bfloat16)
    total = jnp.concatenate([total, rest], axis=1)
    total = after(total, *gathered[rows // 2 + 1 :])

    blocks[:-1] = lax.optimization_barrier((*blocks[:-1], total))[:-1]
    turn = lax.axis_index("col") % steps
    grads = [
        lax.select_n(turn, *(blocks[row_offset(rows, place, t)] for t in range(steps)))
        if 0 < place < rows - 1
        else blocks[place]
        for place in range(rows)
    ]

    starts, stops = [0, 4 * unit, 6 * unit], [4 * unit, 6 * unit, width]
    chunks = range(len(starts))
    came = [[[] for _ in chunks] for _ in range(rows)]
    whole = send(total, 0)
    for chunk in chunks:
        came[rows - 2][chunk].append(whole[:, starts[chunk] : stops[chunk]])

    def message(place, chunk, *before):
        total = product(grads[place], starts[chunk], stops[chunk], *before)
        for block in came[place][chunk]:
            total = total + block.astype(jnp.float32)
        return total.astype(jnp.bfloat16)

    def own_product(chunk, *before):
        return product(grads[0], starts[chunk], stops[chunk], *before)

    for step in range(steps - 1):
        for place in reversed(range(rows - 1)):
            if place & ((1 << step) - 1) or not place >> step & 1:
                continue
            for chunk in chunks:
                total = message(place, chunk, total)
                came[place ^ (1 << step)][chunk].append(send(total, step))
    own = []
    for chunk in chunks:
        total = own_product(chunk, total)
        own.append(total)
    total = message(rows // 2, 0, total)
    last = [send(total, steps - 1)]

    gathered, grads, _ = lax.optimization_barrier((gathered, grads, total))
    grad_weight = lax.dot_general(
        jnp.concatenate(gathered, axis=0),
        jnp.concatenate(grads, axis=0),
        (((0,), (0,)), ((), ())),
        preferred_element_type=jnp.float32,
    )

    total = after(message(rows // 2, 1, grad_weight), *sum(came[0], []))
    last.append(send(total, steps - 1))
    total = after(message(rows // 2, 2, total), last[0])
    last.append(send(total, steps - 1))

    gate_act, up_act = after(gate_act, hidden_came), after(up_act, hidden_came)
    outs = []
    for chunk, start in enumerate(starts):
        outs = finish(
            own[chunk],
            [after(block, grad_weight, *outs) for block in (*came[0][chunk], last[chunk])],
            gate_act,
            up_act,
            outs,
            start,
            math.gcd(unit, 256),
        )
    return (*outs, grad_weight)


def solution(mesh):
    placed = (P("row", "col"), P("row", "col"), P("row", "col"), P("col", "row"))
    return jax.shard_map(
        on_device,
        mesh=mesh,
        in_specs=placed,
        out_specs=(P("row", "col"), P("row", "col"), P("col", "row")),
        check_vma=False,
    )
```

```python
import math

import jax
import jax.numpy as jnp
from jax import lax
from jax.experimental import pallas as pl
from jax.experimental.pallas import tpu as pltpu
from jax.sharding import PartitionSpec as P

BOTH = ("row", "col")


def exchange_pairs(rows, cols, step):
    bits = rows.bit_length() - 1
    return [
        (r * cols + c, (r ^ (1 << ((step + c) % bits))) * cols + c)
        for r in range(rows)
        for c in range(cols)
    ]


def row_offset(rows, place, turn):
    bits = rows.bit_length() - 1
    return sum(1 << ((step + turn) % bits) for step in range(bits) if place >> step & 1)


def spread_tokens(grad_out, hidden, hidden_came, rows, cols):
    share = cols // rows
    part = grad_out.shape[0] // cols
    row, col = lax.axis_index("row"), lax.axis_index("col")
    plane, lane = col // share, col % share

    pieces = grad_out.reshape(rows, share, part, grad_out.shape[1])
    arrived = []
    for shift in range(share):
        piece = lax.dynamic_index_in_dim(pieces, (lane + shift) % share, 1, keepdims=False)
        if shift:
            pairs = [
                (p * share + k, p * share + (k + shift) % share)
                for p in range(rows)
                for k in range(share)
            ]
            piece = lax.ppermute(piece, "col", pairs)
        arrived.append(piece)
    arrived = jnp.stack(arrived)
    mine = jnp.concatenate(
        [
            lax.dynamic_index_in_dim(arrived, (lane - k) % share, 0, keepdims=False)
            for k in range(share)
        ],
        axis=2,
    )

    mine, _ = lax.optimization_barrier((mine, hidden))

    held = []
    for flip in range(rows):
        piece = lax.dynamic_index_in_dim(mine, plane ^ flip, 0, keepdims=False)
        if flip:
            pairs = [(c, (c // share ^ flip) * share + c % share) for c in range(cols)]
            piece = lax.ppermute(piece, "col", pairs)
        held.append(piece)
    held = jnp.stack(held)

    blocks = [None] * rows
    for flip in reversed(range(rows)):
        piece = lax.dynamic_index_in_dim(held, row ^ flip ^ plane, 0, keepdims=False)
        if flip < rows - 1:
            piece = lax.optimization_barrier((piece, blocks[-1]))[0]
        if flip:
            piece = lax.ppermute(piece, "row", [(r, r ^ flip) for r in range(rows)])
        if flip == rows - 1:
            piece = lax.optimization_barrier((piece, hidden_came))[0]
        blocks[flip] = piece
    return blocks


def gather_tokens(blocks, before):
    first = lax.all_gather(blocks[-1], "col", axis=0, tiled=True)
    rest, _ = lax.optimization_barrier((jnp.stack(blocks[:-1]), before))
    rest = lax.all_gather(rest, "col", axis=1, tiled=True)
    return [rest[flip] for flip in range(len(blocks) - 1)] + [first]


def finish_kernel(own_ref, *refs):
    *came_refs, gate_ref, up_ref = refs[: len(refs) - 2]
    gate_out_ref, up_out_ref = refs[-2:]
    grad_hidden = own_ref[...]
    for came_ref in came_refs:
        grad_hidden = grad_hidden + came_ref[...].astype(jnp.float32)
    gate_value = gate_ref[...].astype(jnp.float32)
    up_value = up_ref[...].astype(jnp.float32)
    sigmoid_gate = 0.5 + 0.5 * jnp.tanh(0.5 * gate_value)
    gate_out_ref[...] = (
        grad_hidden * up_value * sigmoid_gate * (1.0 + gate_value * (1.0 - sigmoid_gate))
    ).astype(jnp.bfloat16)
    up_out_ref[...] = (grad_hidden * (gate_value * sigmoid_gate)).astype(jnp.bfloat16)


def finish(own, came, gate_act, up_act, outs, start, block):
    tokens, width = own.shape
    inner = pl.BlockSpec((tokens, block), lambda i: (0, i))
    outer = pl.BlockSpec((tokens, block), lambda i: (0, start // block + i))
    operands = [own, *came, gate_act, up_act]
    specs = [inner] * (1 + len(came)) + [outer] * 2
    kernel, aliases = finish_kernel, {}
    if outs:
        aliases = {len(operands): 0, len(operands) + 1: 1}
        operands += outs
        specs += [pl.BlockSpec(memory_space=pl.ANY)] * 2
        read = len(operands) - 2

        def kernel(*refs):
            finish_kernel(*refs[:read], *refs[read + 2 :])

    shape = jax.ShapeDtypeStruct(gate_act.shape, jnp.bfloat16)
    return pl.pallas_call(
        kernel,
        grid=(width // block,),
        in_specs=specs,
        out_specs=[outer, outer],
        out_shape=[shape, shape],
        input_output_aliases=aliases,
        compiler_params=pltpu.CompilerParams(vmem_limit_bytes=32 * 1024 * 1024),
    )(*operands)


def on_device(grad_out, gate_act, up_act, down_weight):
    rows, cols = lax.axis_size("row"), lax.axis_size("col")
    steps = rows.bit_length() - 1
    tokens = grad_out.shape[0]
    pairs = [exchange_pairs(rows, cols, step) for step in range(steps)]

    def after(value, *others):
        return lax.optimization_barrier((value, *others))[0]

    def activation(gate, up):
        gate = gate.astype(jnp.float32)
        return (gate * jax.nn.sigmoid(gate) * up.astype(jnp.float32)).astype(jnp.bfloat16)

    hidden = activation(gate_act, up_act)
    hidden_came = lax.ppermute(hidden, BOTH, pairs[0])
    pieces = spread_tokens(grad_out, hidden, hidden_came, rows, cols)
    gathered = [hidden, hidden_came]
    for step in range(1, steps - 1):
        gathered = gathered + [lax.ppermute(part, BOTH, pairs[step]) for part in gathered]

    little, large = jnp.split(hidden, [tokens // 8])
    little_came = lax.ppermute(after(little, pieces[-1]), BOTH, pairs[-1])
    large_came = lax.ppermute(after(large, *pieces, little_came), BOTH, pairs[-1])
    gathered.append(jnp.concatenate([little_came, large_came]))

    blocks = gather_tokens(pieces, little_came)
    width = down_weight.shape[0]

    def product(block, start, stop, *before):
        return lax.dot_general(
            after(block, *before),
            down_weight[start:stop],
            (((1,), (1,)), ((), ())),
            preferred_element_type=jnp.float32,
        )

    def send(total, step):
        return lax.ppermute(total, BOTH, pairs[step])

    unit = width // 7
    total = product(blocks[-1], 0, 3 * unit).astype(jnp.bfloat16)
    for part in gathered[1 : rows // 2]:
        gathered.append(send(after(part, total), steps - 1))
    rest = product(blocks[-1], 3 * unit, width, total, large_came).astype(jnp.bfloat16)
    total = jnp.concatenate([total, rest], axis=1)
    total = after(total, *gathered[rows // 2 + 1 :])

    blocks[:-1] = lax.optimization_barrier((*blocks[:-1], total))[:-1]
    turn = lax.axis_index("col") % steps
    grads = [
        lax.select_n(turn, *(blocks[row_offset(rows, place, t)] for t in range(steps)))
        if 0 < place < rows - 1
        else blocks[place]
        for place in range(rows)
    ]

    starts, stops = [0, 4 * unit, 6 * unit], [4 * unit, 6 * unit, width]
    chunks = range(len(starts))
    came = [[[] for _ in chunks] for _ in range(rows)]
    whole = send(total, steps - 1)
    for chunk in chunks:
        came[rows // 2 - 1][chunk].append(whole[:, starts[chunk] : stops[chunk]])

    def message(place, chunk, *before):
        total = product(grads[place], starts[chunk], stops[chunk], *before)
        for block in came[place][chunk]:
            total = total + block.astype(jnp.float32)
        return total.astype(jnp.bfloat16)

    def own_product(chunk, *before):
        return product(grads[0], starts[chunk], stops[chunk], *before)

    for step in reversed(range(1, steps)):
        for place in reversed(range(1 << step, 2 << step)):
            if place == rows - 1:
                continue
            for chunk in chunks:
                total = message(place, chunk, total)
                came[place ^ (1 << step)][chunk].append(send(total, step))
    own = []
    for chunk in chunks:
        total = own_product(chunk, total)
        own.append(total)
    total = message(1, 0, total)
    last = [send(total, 0)]

    gathered, grads, _ = lax.optimization_barrier((gathered, grads, total))
    grad_weight = lax.dot_general(
        jnp.concatenate(gathered, axis=0),
        jnp.concatenate(grads, axis=0),
        (((0,), (0,)), ((), ())),
        preferred_element_type=jnp.float32,
    )

    total = after(message(1, 1, grad_weight), *sum(came[0], []))
    last.append(send(total, 0))
    total = after(message(1, 2, total), last[0])
    last.append(send(total, 0))

    gate_act, up_act = after(gate_act, hidden_came), after(up_act, hidden_came)
    outs = []
    for chunk, start in enumerate(starts):
        outs = finish(
            own[chunk],
            [after(block, grad_weight, *outs) for block in (*came[0][chunk], last[chunk])],
            gate_act,
            up_act,
            outs,
            start,
            math.gcd(unit, 256),
        )
    return (*outs, grad_weight)


def solution(mesh):
    placed = (P("row", "col"), P("row", "col"), P("row", "col"), P("col", "row"))
    return jax.shard_map(
        on_device,
        mesh=mesh,
        in_specs=placed,
        out_specs=(P("row", "col"), P("row", "col"), P("col", "row")),
        check_vma=False,
    )
```

```python
import math

import jax
import jax.numpy as jnp
from jax import lax
from jax.experimental import pallas as pl
from jax.experimental.pallas import tpu as pltpu
from jax.sharding import PartitionSpec as P

BOTH = ("row", "col")


def exchange_pairs(rows, cols, step):
    bits = rows.bit_length() - 1
    return [
        (r * cols + c, (r ^ (1 << ((step + c) % bits))) * cols + c)
        for r in range(rows)
        for c in range(cols)
    ]


def row_offset(rows, place, turn):
    bits = rows.bit_length() - 1
    return sum(1 << ((step + turn) % bits) for step in range(bits) if place >> step & 1)


def spread_tokens(grad_out, hidden, hidden_came, rows, cols):
    share = cols // rows
    part = grad_out.shape[0] // cols
    row, col = lax.axis_index("row"), lax.axis_index("col")
    plane, lane = col // share, col % share

    pieces = grad_out.reshape(rows, share, part, grad_out.shape[1])
    arrived = []
    for shift in range(share):
        piece = lax.dynamic_index_in_dim(pieces, (lane + shift) % share, 1, keepdims=False)
        if shift:
            pairs = [
                (p * share + k, p * share + (k + shift) % share)
                for p in range(rows)
                for k in range(share)
            ]
            piece = lax.ppermute(piece, "col", pairs)
        arrived.append(piece)
    arrived = jnp.stack(arrived)
    mine = jnp.concatenate(
        [
            lax.dynamic_index_in_dim(arrived, (lane - k) % share, 0, keepdims=False)
            for k in range(share)
        ],
        axis=2,
    )

    mine = lax.optimization_barrier((mine, *hidden))[0]

    held = []
    for flip in range(rows):
        piece = lax.dynamic_index_in_dim(mine, plane ^ flip, 0, keepdims=False)
        if flip:
            pairs = [(c, (c // share ^ flip) * share + c % share) for c in range(cols)]
            piece = lax.ppermute(piece, "col", pairs)
        held.append(piece)
    held = jnp.stack(held)

    blocks = [None] * rows
    for flip in reversed(range(rows)):
        piece = lax.dynamic_index_in_dim(held, row ^ flip ^ plane, 0, keepdims=False)
        if flip < rows - 1:
            piece = lax.optimization_barrier((piece, blocks[-1]))[0]
        if flip:
            piece = lax.ppermute(piece, "row", [(r, r ^ flip) for r in range(rows)])
        if flip == rows - 1:
            piece = lax.optimization_barrier((piece, hidden_came))[0]
        blocks[flip] = piece
    return blocks


def gather_tokens(blocks, before):
    first = lax.all_gather(blocks[-1], "col", axis=0, tiled=True)
    rest, _ = lax.optimization_barrier((jnp.stack(blocks[:-1]), before))
    rest = lax.all_gather(rest, "col", axis=1, tiled=True)
    return [rest[flip] for flip in range(len(blocks) - 1)] + [first]


def finish_kernel(own_ref, *refs):
    *came_refs, gate_ref, up_ref = refs[: len(refs) - 2]
    gate_out_ref, up_out_ref = refs[-2:]
    grad_hidden = own_ref[...]
    for came_ref in came_refs:
        grad_hidden = grad_hidden + came_ref[...].astype(jnp.float32)
    gate_value = gate_ref[...].astype(jnp.float32)
    up_value = up_ref[...].astype(jnp.float32)
    sigmoid_gate = 0.5 + 0.5 * jnp.tanh(0.5 * gate_value)
    gate_out_ref[...] = (
        grad_hidden * up_value * sigmoid_gate * (1.0 + gate_value * (1.0 - sigmoid_gate))
    ).astype(jnp.bfloat16)
    up_out_ref[...] = (grad_hidden * (gate_value * sigmoid_gate)).astype(jnp.bfloat16)


def finish(own, came, gate_act, up_act, outs, start, block):
    tokens, width = own.shape
    inner = pl.BlockSpec((tokens, block), lambda i: (0, i))
    outer = pl.BlockSpec((tokens, block), lambda i: (0, start // block + i))
    operands = [own, *came, gate_act, up_act]
    specs = [inner] * (1 + len(came)) + [outer] * 2
    kernel, aliases = finish_kernel, {}
    if outs:
        aliases = {len(operands): 0, len(operands) + 1: 1}
        operands += outs
        specs += [pl.BlockSpec(memory_space=pl.ANY)] * 2
        read = len(operands) - 2

        def kernel(*refs):
            finish_kernel(*refs[:read], *refs[read + 2 :])

    shape = jax.ShapeDtypeStruct(gate_act.shape, jnp.bfloat16)
    return pl.pallas_call(
        kernel,
        grid=(width // block,),
        in_specs=specs,
        out_specs=[outer, outer],
        out_shape=[shape, shape],
        input_output_aliases=aliases,
        compiler_params=pltpu.CompilerParams(vmem_limit_bytes=32 * 1024 * 1024),
    )(*operands)


def on_device(grad_out, gate_act, up_act, down_weight):
    rows, cols = lax.axis_size("row"), lax.axis_size("col")
    steps = rows.bit_length() - 1
    tokens = grad_out.shape[0]
    pairs = [exchange_pairs(rows, cols, step) for step in range(steps)]

    def after(value, *others):
        return lax.optimization_barrier((value, *others))[0]

    def activation(gate, up):
        gate = gate.astype(jnp.float32)
        return (gate * jax.nn.sigmoid(gate) * up.astype(jnp.float32)).astype(jnp.bfloat16)

    hidden = activation(gate_act, up_act)
    hidden_came = lax.ppermute(hidden, BOTH, pairs[0])
    little, large = jnp.split(hidden, [tokens // 8])
    pieces = spread_tokens(grad_out, [hidden, little, large], hidden_came, rows, cols)
    gathered = [hidden, hidden_came]
    for step in range(1, steps - 1):
        gathered = gathered + [lax.ppermute(part, BOTH, pairs[step]) for part in gathered]

    little_came = lax.ppermute(after(little, pieces[-1]), BOTH, pairs[-1])
    large_came = lax.ppermute(after(large, *pieces, little_came), BOTH, pairs[-1])
    gathered.append(jnp.concatenate([little_came, large_came]))

    blocks = gather_tokens(pieces, little_came)
    width = down_weight.shape[0]

    def product(block, start, stop, *before):
        return lax.dot_general(
            after(block, *before),
            down_weight[start:stop],
            (((1,), (1,)), ((), ())),
            preferred_element_type=jnp.float32,
        )

    def send(total, step):
        return lax.ppermute(total, BOTH, pairs[step])

    unit = width // 7
    total = product(blocks[-1], 0, 3 * unit).astype(jnp.bfloat16)
    for part in gathered[1 : rows // 2]:
        gathered.append(send(after(part, total), steps - 1))
    rest = product(blocks[-1], 3 * unit, width, total, large_came).astype(jnp.bfloat16)
    total = jnp.concatenate([total, rest], axis=1)
    total = after(total, *gathered[rows // 2 + 1 :])

    blocks[:-1] = lax.optimization_barrier((*blocks[:-1], total))[:-1]
    turn = lax.axis_index("col") % steps
    grads = [
        lax.select_n(turn, *(blocks[row_offset(rows, place, t)] for t in range(steps)))
        if 0 < place < rows - 1
        else blocks[place]
        for place in range(rows)
    ]

    starts, stops = [0, 4 * unit, 6 * unit], [4 * unit, 6 * unit, width]
    chunks = range(len(starts))
    came = [[[] for _ in chunks] for _ in range(rows)]
    whole = send(total, steps - 1)
    for chunk in chunks:
        came[rows // 2 - 1][chunk].append(whole[:, starts[chunk] : stops[chunk]])

    def message(place, chunk, *before):
        total = product(grads[place], starts[chunk], stops[chunk], *before)
        for block in came[place][chunk]:
            total = total + block.astype(jnp.float32)
        return total.astype(jnp.bfloat16)

    def own_product(chunk, *before):
        return product(grads[0], starts[chunk], stops[chunk], *before)

    for step in reversed(range(1, steps)):
        for place in reversed(range(1 << step, 2 << step)):
            if place == rows - 1:
                continue
            for chunk in chunks:
                total = message(place, chunk, total)
                came[place ^ (1 << step)][chunk].append(send(total, step))
    own = []
    for chunk in chunks:
        total = own_product(chunk, total)
        own.append(total)
    total = message(1, 0, total)
    last = [send(total, 0)]

    gathered, grads, _ = lax.optimization_barrier((gathered, grads, total))
    grad_weight = lax.dot_general(
        jnp.concatenate(gathered, axis=0),
        jnp.concatenate(grads, axis=0),
        (((0,), (0,)), ((), ())),
        preferred_element_type=jnp.float32,
    )

    total = after(message(1, 1, grad_weight), *sum(came[0], []))
    last.append(send(total, 0))
    total = after(message(1, 2, total), last[0])
    last.append(send(total, 0))

    gate_act, up_act = after(gate_act, hidden_came), after(up_act, hidden_came)
    outs = []
    for chunk, start in enumerate(starts):
        outs = finish(
            own[chunk],
            [after(block, grad_weight, *outs) for block in (*came[0][chunk], last[chunk])],
            gate_act,
            up_act,
            outs,
            start,
            math.gcd(unit, 256),
        )
    return (*outs, grad_weight)


def solution(mesh):
    placed = (P("row", "col"), P("row", "col"), P("row", "col"), P("col", "row"))
    return jax.shard_map(
        on_device,
        mesh=mesh,
        in_specs=placed,
        out_specs=(P("row", "col"), P("row", "col"), P("col", "row")),
        check_vma=False,
    )
```

```python
import math

import jax
import jax.numpy as jnp
from jax import lax
from jax.experimental import pallas as pl
from jax.experimental.pallas import tpu as pltpu
from jax.sharding import PartitionSpec as P

BOTH = ("row", "col")


def exchange_pairs(rows, cols, step):
    bits = rows.bit_length() - 1
    return [
        (r * cols + c, (r ^ (1 << ((step + c) % bits))) * cols + c)
        for r in range(rows)
        for c in range(cols)
    ]


def row_offset(rows, place, turn):
    bits = rows.bit_length() - 1
    return sum(1 << ((step + turn) % bits) for step in range(bits) if place >> step & 1)


def spread_tokens(grad_out, hidden, hidden_came, rows, cols):
    share = cols // rows
    part = grad_out.shape[0] // cols
    row, col = lax.axis_index("row"), lax.axis_index("col")
    plane, lane = col // share, col % share

    pieces = grad_out.reshape(rows, share, part, grad_out.shape[1])
    arrived = []
    for shift in range(share):
        piece = lax.dynamic_index_in_dim(pieces, (lane + shift) % share, 1, keepdims=False)
        if shift:
            pairs = [
                (p * share + k, p * share + (k + shift) % share)
                for p in range(rows)
                for k in range(share)
            ]
            piece = lax.ppermute(piece, "col", pairs)
        arrived.append(piece)
    arrived = jnp.stack(arrived)
    mine = jnp.concatenate(
        [
            lax.dynamic_index_in_dim(arrived, (lane - k) % share, 0, keepdims=False)
            for k in range(share)
        ],
        axis=2,
    )

    mine = lax.optimization_barrier((mine, *hidden))[0]

    held = []
    for flip in range(rows):
        piece = lax.dynamic_index_in_dim(mine, plane ^ flip, 0, keepdims=False)
        if flip:
            pairs = [(c, (c // share ^ flip) * share + c % share) for c in range(cols)]
            piece = lax.ppermute(piece, "col", pairs)
        held.append(piece)
    held = jnp.stack(held)

    blocks = [None] * rows
    for flip in reversed(range(rows)):
        piece = lax.dynamic_index_in_dim(held, row ^ flip ^ plane, 0, keepdims=False)
        if flip < rows - 1:
            piece = lax.optimization_barrier((piece, blocks[-1]))[0]
        if flip:
            piece = lax.ppermute(piece, "row", [(r, r ^ flip) for r in range(rows)])
        if flip == rows - 1:
            piece = lax.optimization_barrier((piece, hidden_came))[0]
        blocks[flip] = piece
    return blocks


def gather_tokens(blocks, before):
    first = lax.all_gather(blocks[-1], "col", axis=0, tiled=True)
    rest, _ = lax.optimization_barrier((jnp.stack(blocks[:-1]), before))
    rest = lax.all_gather(rest, "col", axis=1, tiled=True)
    return [rest[flip] for flip in range(len(blocks) - 1)] + [first]


def finish_kernel(own_ref, *refs):
    *came_refs, gate_ref, up_ref = refs[: len(refs) - 2]
    gate_out_ref, up_out_ref = refs[-2:]
    grad_hidden = own_ref[...]
    for came_ref in came_refs:
        grad_hidden = grad_hidden + came_ref[...].astype(jnp.float32)
    gate_value = gate_ref[...].astype(jnp.float32)
    up_value = up_ref[...].astype(jnp.float32)
    sigmoid_gate = 0.5 + 0.5 * jnp.tanh(0.5 * gate_value)
    gate_out_ref[...] = (
        grad_hidden * up_value * sigmoid_gate * (1.0 + gate_value * (1.0 - sigmoid_gate))
    ).astype(jnp.bfloat16)
    up_out_ref[...] = (grad_hidden * (gate_value * sigmoid_gate)).astype(jnp.bfloat16)


def finish(own, came, gate_act, up_act, outs, start, block):
    tokens, width = own.shape
    inner = pl.BlockSpec((tokens, block), lambda i: (0, i))
    outer = pl.BlockSpec((tokens, block), lambda i: (0, start // block + i))
    operands = [own, *came, gate_act, up_act]
    specs = [inner] * (1 + len(came)) + [outer] * 2
    kernel, aliases = finish_kernel, {}
    if outs:
        aliases = {len(operands): 0, len(operands) + 1: 1}
        operands += outs
        specs += [pl.BlockSpec(memory_space=pl.ANY)] * 2
        read = len(operands) - 2

        def kernel(*refs):
            finish_kernel(*refs[:read], *refs[read + 2 :])

    shape = jax.ShapeDtypeStruct(gate_act.shape, jnp.bfloat16)
    return pl.pallas_call(
        kernel,
        grid=(width // block,),
        in_specs=specs,
        out_specs=[outer, outer],
        out_shape=[shape, shape],
        input_output_aliases=aliases,
        compiler_params=pltpu.CompilerParams(vmem_limit_bytes=32 * 1024 * 1024),
    )(*operands)


def on_device(grad_out, gate_act, up_act, down_weight):
    rows, cols = lax.axis_size("row"), lax.axis_size("col")
    steps = rows.bit_length() - 1
    tokens = grad_out.shape[0]
    pairs = [exchange_pairs(rows, cols, step) for step in range(steps)]

    def after(value, *others):
        return lax.optimization_barrier((value, *others))[0]

    def activation(gate, up):
        gate = gate.astype(jnp.float32)
        return (gate * jax.nn.sigmoid(gate) * up.astype(jnp.float32)).astype(jnp.bfloat16)

    hidden = activation(gate_act, up_act)
    hidden_came = lax.ppermute(hidden, BOTH, pairs[0])
    little, large = jnp.split(hidden, [tokens // 8])
    pieces = spread_tokens(grad_out, [hidden, little, large], hidden_came, rows, cols)
    gathered = [hidden, hidden_came]
    for step in range(1, steps - 1):
        gathered = gathered + [lax.ppermute(part, BOTH, pairs[step]) for part in gathered]

    little_came = lax.ppermute(after(little, pieces[-1]), BOTH, pairs[-1])
    large_came = lax.ppermute(after(large, *pieces, little_came), BOTH, pairs[-1])
    gathered.append(jnp.concatenate([little_came, large_came]))

    blocks = gather_tokens(pieces, little_came)
    width = down_weight.shape[0]

    def product(block, start, stop, *before):
        return lax.dot_general(
            after(block, *before),
            down_weight[start:stop],
            (((1,), (1,)), ((), ())),
            preferred_element_type=jnp.float32,
        )

    def send(total, step):
        return lax.ppermute(total, BOTH, pairs[step])

    unit = width // 7
    total = product(blocks[-1], 0, 3 * unit).astype(jnp.bfloat16)
    for part in gathered[1 : rows // 2]:
        gathered.append(send(after(part, total), steps - 1))
    rest = product(blocks[-1], 3 * unit, width, total, large_came).astype(jnp.bfloat16)
    total = jnp.concatenate([total, rest], axis=1)
    total = after(total, *gathered[rows // 2 + 1 :])

    blocks[:-1] = lax.optimization_barrier((*blocks[:-1], total))[:-1]
    turn = lax.axis_index("col") % steps
    grads = [
        lax.select_n(turn, *(blocks[row_offset(rows, place, t)] for t in range(steps)))
        if 0 < place < rows - 1
        else blocks[place]
        for place in range(rows)
    ]

    starts, stops = [0, 4 * unit, 6 * unit], [4 * unit, 6 * unit, width]
    chunks = range(len(starts))
    came = [[[] for _ in chunks] for _ in range(rows)]
    whole = send(total, steps - 1)
    for chunk in chunks:
        came[rows // 2 - 1][chunk].append(whole[:, starts[chunk] : stops[chunk]])

    def message(place, chunk, step, *before):
        total = product(grads[place], starts[chunk], stops[chunk], *before)
        for block in came[place][chunk]:
            total = total + block.astype(jnp.float32)
        return total.astype(jnp.bfloat16 if step >= steps - 2 else jnp.float32)

    def own_product(chunk, *before):
        return product(grads[0], starts[chunk], stops[chunk], *before)

    for step in reversed(range(1, steps)):
        for place in reversed(range(1 << step, 2 << step)):
            if place == rows - 1:
                continue
            for chunk in chunks:
                total = message(place, chunk, step, total)
                came[place ^ (1 << step)][chunk].append(send(total, step))
    own = []
    for chunk in chunks:
        total = own_product(chunk, total)
        own.append(total)
    total = message(1, 0, 0, total)
    last = [send(total, 0)]

    gathered, grads, _ = lax.optimization_barrier((gathered, grads, total))
    grad_weight = lax.dot_general(
        jnp.concatenate(gathered, axis=0),
        jnp.concatenate(grads, axis=0),
        (((0,), (0,)), ((), ())),
        preferred_element_type=jnp.float32,
    )

    total = after(message(1, 1, 0, grad_weight), *sum(came[0], []))
    last.append(send(total, 0))
    total = after(message(1, 2, 0, total), last[0])
    last.append(send(total, 0))

    gate_act, up_act = after(gate_act, hidden_came), after(up_act, hidden_came)
    outs = []
    for chunk, start in enumerate(starts):
        outs = finish(
            own[chunk],
            [after(block, grad_weight, *outs) for block in (*came[0][chunk], last[chunk])],
            gate_act,
            up_act,
            outs,
            start,
            math.gcd(unit, 256),
        )
    return (*outs, grad_weight)


def solution(mesh):
    placed = (P("row", "col"), P("row", "col"), P("row", "col"), P("col", "row"))
    return jax.shard_map(
        on_device,
        mesh=mesh,
        in_specs=placed,
        out_specs=(P("row", "col"), P("row", "col"), P("col", "row")),
        check_vma=False,
    )
```

```python
import math

import jax
import jax.numpy as jnp
from jax import lax
from jax.experimental import pallas as pl
from jax.experimental.pallas import tpu as pltpu
from jax.sharding import PartitionSpec as P

BOTH = ("row", "col")


def exchange_pairs(rows, cols, step):
    bits = rows.bit_length() - 1
    return [
        (r * cols + c, (r ^ (1 << ((step + c) % bits))) * cols + c)
        for r in range(rows)
        for c in range(cols)
    ]


def row_offset(rows, place, turn):
    bits = rows.bit_length() - 1
    return sum(1 << ((step + turn) % bits) for step in range(bits) if place >> step & 1)


def spread_tokens(grad_out, hidden, hidden_came, rows, cols):
    share = cols // rows
    part = grad_out.shape[0] // cols
    row, col = lax.axis_index("row"), lax.axis_index("col")
    plane, lane = col // share, col % share

    pieces = grad_out.reshape(rows, share, part, grad_out.shape[1])
    arrived = []
    for shift in range(share):
        piece = lax.dynamic_index_in_dim(pieces, (lane + shift) % share, 1, keepdims=False)
        if shift:
            pairs = [
                (p * share + k, p * share + (k + shift) % share)
                for p in range(rows)
                for k in range(share)
            ]
            piece = lax.ppermute(piece, "col", pairs)
        arrived.append(piece)
    arrived = jnp.stack(arrived)
    mine = jnp.concatenate(
        [
            lax.dynamic_index_in_dim(arrived, (lane - k) % share, 0, keepdims=False)
            for k in range(share)
        ],
        axis=2,
    )

    mine = lax.optimization_barrier((mine, *hidden))[0]

    held = []
    for flip in range(rows):
        piece = lax.dynamic_index_in_dim(mine, plane ^ flip, 0, keepdims=False)
        if flip:
            pairs = [(c, (c // share ^ flip) * share + c % share) for c in range(cols)]
            piece = lax.ppermute(piece, "col", pairs)
        held.append(piece)
    held = jnp.stack(held)

    blocks = [None] * rows
    for flip in reversed(range(rows)):
        piece = lax.dynamic_index_in_dim(held, row ^ flip ^ plane, 0, keepdims=False)
        if flip < rows - 1:
            piece = lax.optimization_barrier((piece, blocks[-1]))[0]
        if flip:
            piece = lax.ppermute(piece, "row", [(r, r ^ flip) for r in range(rows)])
        if flip == rows - 1:
            piece = lax.optimization_barrier((piece, hidden_came))[0]
        blocks[flip] = piece
    return blocks


def gather_tokens(blocks, before):
    first = lax.all_gather(blocks[-1], "col", axis=0, tiled=True)
    rest, _ = lax.optimization_barrier((jnp.stack(blocks[:-1]), before))
    rest = lax.all_gather(rest, "col", axis=1, tiled=True)
    return [rest[flip] for flip in range(len(blocks) - 1)] + [first]


def finish_kernel(own_ref, *refs):
    *came_refs, gate_ref, up_ref = refs[: len(refs) - 2]
    gate_out_ref, up_out_ref = refs[-2:]
    grad_hidden = own_ref[...]
    for came_ref in came_refs:
        grad_hidden = grad_hidden + came_ref[...].astype(jnp.float32)
    gate_value = gate_ref[...].astype(jnp.float32)
    up_value = up_ref[...].astype(jnp.float32)
    sigmoid_gate = 0.5 + 0.5 * jnp.tanh(0.5 * gate_value)
    gate_out_ref[...] = (
        grad_hidden * up_value * sigmoid_gate * (1.0 + gate_value * (1.0 - sigmoid_gate))
    ).astype(jnp.bfloat16)
    up_out_ref[...] = (grad_hidden * (gate_value * sigmoid_gate)).astype(jnp.bfloat16)


def finish(own, came, gate_act, up_act, outs, start, block):
    tokens, width = own.shape
    inner = pl.BlockSpec((tokens, block), lambda i: (0, i))
    outer = pl.BlockSpec((tokens, block), lambda i: (0, start // block + i))
    operands = [own, *came, gate_act, up_act]
    specs = [inner] * (1 + len(came)) + [outer] * 2
    kernel, aliases = finish_kernel, {}
    if outs:
        aliases = {len(operands): 0, len(operands) + 1: 1}
        operands += outs
        specs += [pl.BlockSpec(memory_space=pl.ANY)] * 2
        read = len(operands) - 2

        def kernel(*refs):
            finish_kernel(*refs[:read], *refs[read + 2 :])

    shape = jax.ShapeDtypeStruct(gate_act.shape, jnp.bfloat16)
    return pl.pallas_call(
        kernel,
        grid=(width // block,),
        in_specs=specs,
        out_specs=[outer, outer],
        out_shape=[shape, shape],
        input_output_aliases=aliases,
        compiler_params=pltpu.CompilerParams(vmem_limit_bytes=32 * 1024 * 1024),
    )(*operands)


def on_device(grad_out, gate_act, up_act, down_weight):
    rows, cols = lax.axis_size("row"), lax.axis_size("col")
    steps = rows.bit_length() - 1
    tokens = grad_out.shape[0]
    pairs = [exchange_pairs(rows, cols, step) for step in range(steps)]

    def after(value, *others):
        return lax.optimization_barrier((value, *others))[0]

    def activation(gate, up):
        gate = gate.astype(jnp.float32)
        return (gate * jax.nn.sigmoid(gate) * up.astype(jnp.float32)).astype(jnp.bfloat16)

    hidden = activation(gate_act, up_act)
    hidden_came = lax.ppermute(hidden, BOTH, pairs[0])
    little, large = jnp.split(hidden, [tokens // 8])
    pieces = spread_tokens(grad_out, [hidden, little, large], hidden_came, rows, cols)
    gathered = [hidden, hidden_came]
    for step in range(1, steps - 1):
        gathered = gathered + [lax.ppermute(part, BOTH, pairs[step]) for part in gathered]

    little_came = lax.ppermute(after(little, pieces[-1]), BOTH, pairs[-1])
    large_came = lax.ppermute(after(large, *pieces, little_came), BOTH, pairs[-1])
    gathered.append(jnp.concatenate([little_came, large_came]))

    blocks = gather_tokens(pieces, little_came)
    width = down_weight.shape[0]

    def product(block, start, stop, *before):
        return lax.dot_general(
            after(block, *before),
            down_weight[start:stop],
            (((1,), (1,)), ((), ())),
            preferred_element_type=jnp.float32,
        )

    def send(total, step):
        return lax.ppermute(total, BOTH, pairs[step])

    unit = width // 7
    total = product(blocks[-1], 0, 3 * unit).astype(jnp.bfloat16)
    for part in gathered[1 : rows // 2]:
        gathered.append(send(after(part, total), steps - 1))
    rest = product(blocks[-1], 3 * unit, width, total, large_came).astype(jnp.bfloat16)
    total = jnp.concatenate([total, rest], axis=1)
    total = after(total, *gathered[rows // 2 + 1 :])

    blocks[:-1] = lax.optimization_barrier((*blocks[:-1], total))[:-1]
    turn = lax.axis_index("col") % steps
    grads = [
        lax.select_n(turn, *(blocks[row_offset(rows, place, t)] for t in range(steps)))
        if 0 < place < rows - 1
        else blocks[place]
        for place in range(rows)
    ]

    starts, stops = [0, 4 * unit, 6 * unit], [4 * unit, 6 * unit, width]
    chunks = range(len(starts))
    came = [[[] for _ in chunks] for _ in range(rows)]
    whole = send(total, steps - 1)
    for chunk in chunks:
        came[rows // 2 - 1][chunk].append(whole[:, starts[chunk] : stops[chunk]])

    def message(place, chunk, step, *before):
        total = product(grads[place], starts[chunk], stops[chunk], *before)
        for block in came[place][chunk]:
            total = total + block.astype(jnp.float32)
        return total.astype(jnp.bfloat16 if step >= steps - 2 else jnp.float32)

    def own_product(chunk, *before):
        return product(grads[0], starts[chunk], stops[chunk], *before)

    for step in reversed(range(1, steps)):
        for place in reversed(range(1 << step, 2 << step)):
            if place == rows - 1:
                continue
            for chunk in chunks:
                total = message(place, chunk, step, total)
                came[place ^ (1 << step)][chunk].append(send(total, step))
    own = []
    for chunk in chunks:
        total = own_product(chunk, total)
        own.append(total)
    total = message(1, 0, 0, total)
    last = [send(total, 0)]

    gathered, grads, _ = lax.optimization_barrier((gathered, grads, total))
    grad_weight = lax.dot_general(
        jnp.concatenate(gathered, axis=0),
        jnp.concatenate(grads, axis=0),
        (((0,), (0,)), ((), ())),
        preferred_element_type=jnp.float32,
    )

    total = after(message(1, 1, 0, grad_weight), *sum(came[0], []))
    last.append(send(total, 0))
    total = after(message(1, 2, 0, total), last[0])
    last.append(send(total, 0))

    gate_act, up_act = after(gate_act, hidden_came), after(up_act, hidden_came)
    outs = []
    for chunk, start in enumerate(starts):
        outs = finish(
            own[chunk],
            [after(block, grad_weight, *outs) for block in (*came[0][chunk], last[chunk])],
            gate_act,
            up_act,
            outs,
            start,
            math.gcd(unit, 512),
        )
    return (*outs, grad_weight)


def solution(mesh):
    placed = (P("row", "col"), P("row", "col"), P("row", "col"), P("col", "row"))
    return jax.shard_map(
        on_device,
        mesh=mesh,
        in_specs=placed,
        out_specs=(P("row", "col"), P("row", "col"), P("col", "row")),
        check_vma=False,
    )
```
